256 devices in a mesh: ctx: 32 (over x_lo, z, core), head: 8 (over x_hi, y).
Axes of the slice: x: 4 (x_hi: 2, x_lo: 2; x = x_hi * 2 + x_lo), y: 4, z: 8, core: 2. Of those that a mesh axis runs over, the one named last changes fastest.
Arguments:
- tokens: bfloat16 [4096, 5120], P('ctx', 'head'), may hold values from -6 to 6
- kv_values: bfloat16 [2560, 576], P('head'), may hold values from -0.125 to 0.125
- kv_pattern: int32 [1280, 576], P('head'), may hold values from 0 to 5
- kv_down: bfloat16 [5120, 16], P('head'), may hold values from -0.078125 to 0.078125
- kv_up: bfloat16 [16, 576], replicated, may hold values from -1.5 to 1.5
- kv_gain: float32 [512], replicated, may hold values from 0.5 to 1.5
- queries: bfloat16 [4096, 64, 192], P('ctx', 'head'), may hold values from -110 to 110
- absorb_k: bfloat16 [64, 128, 512], P('head'), may hold values from -0.5 to 0.5
- absorb_v: bfloat16 [64, 512, 128], P('head'), may hold values from -0.25 to 0.25
- o_values: bfloat16 [4096, 2560], P('head'), may hold values from -0.09375 to 0.09375
- o_pattern: int32 [2048, 2560], P('head'), may hold values from 0 to 5
- o_down: bfloat16 [8192, 16], P('head'), may hold values from -0.0625 to 0.0625
- o_up: bfloat16 [16, 2560], replicated, may hold values from -1.5 to 1.5
Outputs:
- mixed: float32 [4096, 2560], P('ctx', 'head')
The draws below stay inside these ranges and needn't reach their ends.
All inputs are finite; a program needn't handle non-finite values.
Results may differ from the reference program's by a relative error of at most 0.01265.
The reference program's roundings to bfloat16 on the way count: a program that leaves them out, or rounds other values in their place, can miss the bound.
Values may be sent and summed in bfloat16 or wider, within the bound.
No kernel may reach another device: no remote copies, remote signals or barrier semaphores. Data moves between devices by JAX's collectives and lax.ppermute only.
A program may use at most 128 MiB of HBM per device.

```python
import math
import jax
import jax.numpy as jnp
from jax import lax

D = 5120
LAT = 512
ROPE = 64
NOPE = 128
VDIM = 128
H = 64
DO = 2560
RANK = 16
TOKENS = 4096


def draw_queries(key, part):
    key = jax.random.fold_in(key, 11)
    shape = (TOKENS, H, NOPE + ROPE)
    values = jnp.clip(jax.random.normal(key, shape, jnp.float32), -6.0, 6.0)
    return values.astype(jnp.bfloat16)


def place_ends(array, key, smallest, largest):
    shape = array.shape
    index_at = [jax.random.randint(jax.random.fold_in(key, axis), (), 0, shape[axis]) for axis in range(len(shape))]
    array = array.at[tuple(index_at)].set(smallest)
    longest = shape.index(max(shape))
    index_at[longest] = (index_at[longest] + 1) % shape[longest]
    return array.at[tuple(index_at)].set(largest)


def levels(stream_key, dims, shards, least, top_value):
    level, own = 1.0, jax.random.fold_in(stream_key, 6)
    for dim, parts in shards:
        steps = jnp.exp(jax.random.uniform(jax.random.fold_in(own, dim), (parts,), jnp.float32, least / len(shards), top_value / len(shards)))
        level = level * jnp.repeat(steps, dims[dim] // parts).reshape([-1 if axis == dim else 1 for axis in range(len(dims))])
    return level


def bell_draw(own_key, dims, scale, reach, cuts=(), kind=jnp.bfloat16):
    loudness = levels(own_key, dims, cuts, -0.22, 0.18) if cuts else 1.0
    result = jax.random.normal(own_key, dims, jnp.float32) * scale * loudness
    return jnp.minimum(jnp.maximum(result, -reach), reach).astype(kind)


def setup_inputs(seed: int = 0) -> dict:
    seeds = jax.random.split(jax.random.key(seed), 14)
    tokens = bell_draw(seeds[0], (TOKENS, D), 1.0, 6.0, ((0, 32), (1, 8)))
    kv_values = bell_draw(seeds[1], (D // 2, LAT + ROPE), (D // 2) ** -0.5, 0.125, ((0, 8),))
    kv_pattern = place_ends(jax.random.randint(seeds[2], (D // 4, LAT + ROPE), 0, 6), jax.random.fold_in(seeds[2], 1), 0, 5).astype(jnp.int32)
    kv_down = bell_draw(seeds[3], (D, RANK), D ** -0.5, 0.078125, ((0, 8),))
    kv_up = bell_draw(seeds[4], (RANK, LAT + ROPE), RANK ** -0.5, 1.5)
    kv_gain = jnp.clip(1.0 + 0.1 * jax.random.normal(seeds[5], (LAT,), jnp.float32), 0.5, 1.5)
    queries = draw_queries(jax.random.fold_in(seeds[13], 71), 0)
    absorb_k = bell_draw(seeds[7], (H, NOPE, LAT), NOPE ** -0.5, 0.5, ((0, 8),))
    absorb_v = bell_draw(seeds[8], (H, LAT, VDIM), LAT ** -0.5, 0.25, ((0, 8),))
    o_values = bell_draw(seeds[9], (H * VDIM // 2, DO), (H * VDIM // 2) ** -0.5, 0.09375, ((0, 8),))
    o_pattern = place_ends(jax.random.randint(seeds[10], (H * VDIM // 4, DO), 0, 6), jax.random.fold_in(seeds[10], 1), 0, 5).astype(jnp.int32)
    o_down = bell_draw(seeds[11], (H * VDIM, RANK), (H * VDIM) ** -0.5, 0.0625, ((0, 8),))
    o_up = bell_draw(seeds[12], (RANK, DO), RANK ** -0.5, 1.5)
    return {"tokens": tokens, "kv_values": kv_values, "kv_pattern": kv_pattern, "kv_down": kv_down, "kv_up": kv_up, "kv_gain": kv_gain, "queries": queries, "absorb_k": absorb_k, "absorb_v": absorb_v, "o_values": o_values, "o_pattern": o_pattern, "o_down": o_down, "o_up": o_up}


def densify(values, pattern):
    groups = pattern.shape[0]
    columns = values.shape[1]
    pairs = values.reshape(groups, 2, columns)
    upper = (pattern >= 3).astype(jnp.int32)
    topmost = (pattern >= 5).astype(jnp.int32)
    first = upper + topmost
    second = pattern + 1 - 2 * upper - topmost
    slots = jnp.arange(4, dtype=jnp.int32)[None, :, None]
    nothing = jnp.zeros((), values.dtype)
    dense = jnp.where(slots == first[:, None, :], pairs[:, 0:1, :], nothing) + jnp.where(slots == second[:, None, :], pairs[:, 1:2, :], nothing)
    return dense.reshape(groups * 4, columns)

def rotate(vector, positions):
    half_width = vector.shape[-1] // 2
    freqs = 10000.0 ** (-jnp.arange(half_width, dtype=jnp.float32) / half_width)
    angles = positions.astype(jnp.float32)[..., None] * freqs
    lower = vector[..., :half_width]
    higher = vector[..., half_width:]
    return jnp.concatenate([lower * jnp.cos(angles) - higher * jnp.sin(angles), higher * jnp.cos(angles) + lower * jnp.sin(angles)], axis=-1)

def finish_cache(raw, positions, gain, width):
    latent = raw[:, :width]
    meansq = lax.optimization_barrier(jnp.mean(latent * latent, axis=-1, keepdims=True))
    normed = latent * lax.rsqrt(meansq + 1e-06) * gain
    return jnp.concatenate([normed, rotate(raw[:, width:], positions)], axis=1).astype(jnp.bfloat16)

def reference(tokens, kv_values, kv_pattern, kv_down, kv_up, kv_gain, queries, absorb_k, absorb_v, o_values, o_pattern, o_down, o_up):
    kv_dense = densify(kv_values, kv_pattern)
    lowrank = jnp.dot(tokens, kv_down, preferred_element_type=jnp.float32)
    raw = jnp.dot(tokens, kv_dense, preferred_element_type=jnp.float32) + jnp.dot(lowrank, kv_up.astype(jnp.float32), precision=lax.Precision.HIGHEST)
    positions = jnp.arange(TOKENS, dtype=jnp.int32)
    cache = finish_cache(raw, positions, kv_gain, LAT)
    score_scale = 1.0 / math.sqrt(NOPE + ROPE)
    block = min(1024, TOKENS)

    def one_head(inputs):
        query_head, key_weight, value_weight = inputs
        latent_query = jnp.dot(query_head[:, :NOPE], key_weight, preferred_element_type=jnp.float32).astype(jnp.bfloat16)
        rope_query = rotate(query_head[:, NOPE:].astype(jnp.float32), positions).astype(jnp.bfloat16)
        full_query = jnp.concatenate([latent_query, rope_query], axis=1)
        outputs = []
        for number in range(TOKENS // block):
            begin = number * block
            stop = begin + block
            keys = cache[:stop]
            scores = jnp.dot(full_query[begin:stop], keys.T, preferred_element_type=jnp.float32) * score_scale
            visible = positions[None, :stop] <= positions[begin:stop, None]
            scores = jnp.where(visible, scores, -jnp.inf)
            weights = jax.nn.softmax(scores, axis=-1).astype(jnp.bfloat16)
            outputs.append(jnp.dot(weights, keys[:, :LAT], preferred_element_type=jnp.float32))
        attended = jnp.concatenate(outputs, axis=0).astype(jnp.bfloat16)
        return jnp.dot(attended, value_weight, preferred_element_type=jnp.float32).astype(jnp.bfloat16)
    head_out = lax.map(one_head, (jnp.transpose(queries, (1, 0, 2)), absorb_k, absorb_v))
    flat = jnp.transpose(head_out, (1, 0, 2)).reshape(TOKENS, H * VDIM)
    o_dense = densify(o_values, o_pattern)
    adapter = jnp.dot(flat, o_down, preferred_element_type=jnp.float32)
    mixed = jnp.dot(flat, o_dense, preferred_element_type=jnp.float32) + jnp.dot(adapter, o_up.astype(jnp.float32), precision=lax.Precision.HIGHEST)
    return mixed
```

```python
import functools
import math

import jax
import jax.numpy as jnp
from jax import lax
from jax.experimental import pallas as pl
from jax.experimental.pallas import tpu as pltpu
from jax.sharding import PartitionSpec as P

BF16 = jnp.bfloat16
F32 = jnp.float32
MIB = 1024 * 1024
HEADS = 8
ROWS = 128
PIECE = ROWS // HEADS
LAT = 512
ROPE = 64
WIDTH = LAT + ROPE
NOPE = 128
VDIM = 128
CHIPS = 16
GROUP = 4
KEYS = GROUP * ROWS
BLOCK = 256
COLS = 640
LOG2E = 1.4426950408889634


def dot(a, b):
    return jnp.dot(a, b, preferred_element_type=F32)


def one_hot(shape, column_of_row):
    rows = lax.broadcasted_iota(jnp.int32, shape, 0)
    columns = lax.broadcasted_iota(jnp.int32, shape, 1)
    return jnp.where(columns == column_of_row(rows), 1.0, 0.0).astype(BF16)


def unpair(count):
    half = count // 2
    return one_hot((count, count), lambda r: jnp.where(r < half, 2 * r, 2 * (r - half) + 1))


def by_slot():
    rows = lax.broadcasted_iota(jnp.int32, (128, 128), 0)
    columns = lax.broadcasted_iota(jnp.int32, (128, 128), 1)
    return jnp.where(rows == 4 * (columns % 32) + columns // 32, 1.0, 0.0).astype(BF16)


def densify(values_ref, pattern_ref, dense_ref):
    total = values_ref.shape[0]
    begin = 0
    while begin < total:
        count = min(256, total - begin)
        half = count // 2
        pair = dot(unpair(count), values_ref[begin : begin + count, :])
        v0, v1 = pair[:half], pair[half:]
        p = pattern_ref[begin // 2 : begin // 2 + half, :]
        slots = (
            jnp.where(p < 3, v0, 0.0),
            jnp.where(p == 0, v1, jnp.where((p == 3) | (p == 4), v0, 0.0)),
            jnp.where((p == 1) | (p == 3), v1, jnp.where(p == 5, v0, 0.0)),
            jnp.where((p == 2) | (p >= 4), v1, 0.0),
        )
        for k, slot in enumerate(slots):
            slot = slot.astype(BF16)
            for b in range(half // 32):
                row = 2 * begin + 128 * b + 32 * k
                dense_ref[row : row + 32, :] = slot[32 * b : 32 * b + 32]
        begin += count


def thirds(x):
    high = x.astype(BF16)
    rest = x - high.astype(F32)
    middle = rest.astype(BF16)
    low = (rest - middle.astype(F32)).astype(BF16)
    return high, middle, low


def turn(x, table):
    half = ROPE // 2
    swapped = jnp.concatenate([x[:, half:], x[:, :half]], axis=1)
    return x * table[:, :ROPE] + swapped * table[:, ROPE:]


def project_kernel(tokens_ref, values_ref, pattern_ref, down_ref, up_ref, raw_ref, dense_ref):
    densify(values_ref, pattern_ref, dense_ref)
    order = by_slot()
    tokens = tokens_ref[...]
    parts = [dot(tokens[:, b : b + 128], order).astype(BF16) for b in range(0, tokens.shape[1], 128)]
    raw = dot(jnp.concatenate(parts, axis=1), dense_ref[...])
    up = up_ref[...]
    for term in thirds(dot(tokens, down_ref[...])):
        raw += dot(term, up)
    raw_ref[...] = raw.reshape(raw_ref.shape)


def query_kernel(queries_ref, absorb_ref, table_ref, out_ref):
    table = table_ref[...]
    for h in range(HEADS):
        rows = slice(h * ROWS, (h + 1) * ROWS)
        out_ref[rows, :LAT] = dot(queries_ref[h, :, :NOPE], absorb_ref[h]).astype(BF16)
        out_ref[rows, LAT:] = turn(queries_ref[h, :, NOPE:].astype(F32), table).astype(BF16)


def finish_kernel(where_ref, parts_ref, gain_ref, table_ref, out_ref):
    raw = parts_ref[0]
    for h in range(1, HEADS):
        raw += parts_ref[h]
    latent = raw[:, :LAT]
    meansq = jnp.mean(latent * latent, axis=-1, keepdims=True)
    normed = (latent * lax.rsqrt(meansq + 1e-06) * gain_ref[...]).astype(BF16)
    table = table_ref[pl.ds(pl.multiple_of(where_ref[2] * PIECE, PIECE), PIECE), :]
    turned = turn(raw[:, LAT:], table).astype(BF16)
    for c in range(CHIPS):
        out_ref[c, :, :LAT] = normed
        out_ref[c, :, LAT:] = turned


def attend(where_ref, q_ref, keys_ref, m_ref, l_ref, acc_ref, key_core, scale):
    chip, core = where_ref[0], where_ref[1]

    def chunk(j, masked):
        keys = jnp.concatenate(
            [keys_ref[:, GROUP * j + b].reshape(ROWS, WIDTH) for b in range(GROUP)], axis=0
        )
        if masked:
            row = lax.broadcasted_iota(jnp.int32, (BLOCK, KEYS), 0) % ROWS
            column = lax.broadcasted_iota(jnp.int32, (BLOCK, KEYS), 1)
            ahead = (2 * chip + core) * ROWS + row
            place = (2 * (GROUP * j + column // ROWS) + key_core) * ROWS + column % ROWS
            visible = place <= ahead
        for b in range(HEADS * ROWS // BLOCK):
            rows = slice(b * BLOCK, (b + 1) * BLOCK)
            scores = lax.dot_general(
                q_ref[rows, :], keys, (((1,), (1,)), ((), ())), preferred_element_type=F32
            ) * scale
            if masked:
                scores = jnp.where(visible, scores, -jnp.inf)
            old = m_ref[rows, :]
            new = jnp.maximum(old, jnp.max(scores, axis=1, keepdims=True))
            factor = jnp.exp2(old - new)
            weights = jnp.exp2(scores - jnp.concatenate([new] * (KEYS // 128), axis=1))
            part = weights[:, :128]
            for c in range(128, KEYS, 128):
                part += weights[:, c : c + 128]
            m_ref[rows, :] = new
            l_ref[rows, :] = l_ref[rows, :] * factor + part
            acc_ref[rows, :] = acc_ref[rows, :] * jnp.concatenate(
                [factor] * (LAT // 128), axis=1
            ) + dot(weights.astype(BF16), keys[:, :LAT])

    last = chip // GROUP

    @pl.loop(0, last)
    def _(j):
        chunk(j, False)

    chunk(last, True)


def first_kernel(scale, where_ref, q_ref, keys_ref, m_ref, l_ref, acc_ref):
    m_ref[...] = jnp.full(m_ref.shape, -jnp.inf, F32)
    l_ref[...] = jnp.zeros(l_ref.shape, F32)
    acc_ref[...] = jnp.zeros(acc_ref.shape, F32)
    attend(where_ref, q_ref, keys_ref, m_ref, l_ref, acc_ref, where_ref[1], scale)


def second_kernel(
    scale, where_ref, q_ref, keys_ref, m_in, l_in, acc_in, absorb_ref, down_ref,
    flat_ref, low_ref, m_ref, l_ref, acc_ref,
):
    m_ref[...] = m_in[...]
    l_ref[...] = l_in[...]
    acc_ref[...] = acc_in[...]
    attend(where_ref, q_ref, keys_ref, m_ref, l_ref, acc_ref, 1 - where_ref[1], scale)
    order = by_slot()
    lowrank = jnp.zeros((ROWS, down_ref.shape[1]), F32)
    for h in range(HEADS):
        rows = slice(h * ROWS, (h + 1) * ROWS)
        total = jnp.sum(l_ref[rows, :], axis=1, keepdims=True)
        attended = (acc_ref[rows, :] / total).astype(BF16)
        out = dot(attended, absorb_ref[h]).astype(BF16)
        lowrank += dot(out, down_ref[h * VDIM : (h + 1) * VDIM, :])
        flat_ref[:, h * VDIM : (h + 1) * VDIM] = dot(out, order).astype(BF16)
    for n, term in enumerate(thirds(lowrank)):
        low_ref[n] = term


def output_kernel(flat_ref, low_ref, values_ref, pattern_ref, up_ref, out_ref, dense_ref):
    densify(values_ref, pattern_ref, dense_ref)
    terms = dot(flat_ref[...], dense_ref[...])
    up = up_ref[...]
    for n in range(3):
        terms += dot(low_ref[n], up)
    out_ref[...] = terms.T.astype(BF16)


def sum_kernel(parts_ref, out_ref):
    total = parts_ref[0].astype(F32)
    for h in range(1, HEADS):
        total += parts_ref[h].astype(F32)
    out_ref[...] = total.T


def shape(*dims, dtype=F32):
    return jax.ShapeDtypeStruct(dims, dtype)


def params(mib):
    return pltpu.CompilerParams(vmem_limit_bytes=mib * MIB)


VMEM = pl.BlockSpec(memory_space=pltpu.VMEM)
SMEM = pl.BlockSpec(memory_space=pltpu.SMEM)


def local(
    tokens, kv_values, kv_pattern, kv_down, kv_up, kv_gain, queries, absorb_k, absorb_v,
    o_values, o_pattern, o_down, o_up,
):
    ctx = lax.axis_index("ctx")
    head = lax.axis_index("head")
    where = jnp.stack([ctx // 2, ctx % 2, head]).astype(jnp.int32)
    scale = LOG2E / math.sqrt(queries.shape[2])
    out_cols = o_values.shape[1]

    raw = pl.pallas_call(
        project_kernel,
        out_shape=shape(HEADS, PIECE, WIDTH),
        in_specs=[VMEM] * 5,
        out_specs=VMEM,
        scratch_shapes=[pltpu.VMEM((tokens.shape[1], WIDTH), BF16)],
        compiler_params=params(24),
        name="project",
    )(tokens, kv_values, kv_pattern, kv_down, kv_up)
    parts = lax.all_to_all(raw, "head", 0, 0, tiled=True)

    half = ROPE // 2
    freqs = 10000.0 ** (-jnp.arange(half, dtype=F32) / half)
    positions = ctx * ROWS + jnp.arange(ROWS, dtype=jnp.int32)
    angles = positions.astype(F32)[:, None] * freqs
    cos, sin = jnp.cos(angles), jnp.sin(angles)
    table = jnp.concatenate([cos, cos, -sin, sin], axis=1)

    piece = pl.pallas_call(
        finish_kernel,
        out_shape=shape(CHIPS, PIECE, WIDTH, dtype=BF16),
        in_specs=[SMEM, VMEM, VMEM, VMEM],
        out_specs=VMEM,
        compiler_params=params(24),
        name="finish",
    )(where, parts, kv_gain.reshape(1, LAT), table)

    chips = [[2 * chip + core for chip in range(CHIPS)] for core in range(2)]
    column = lax.all_to_all(piece, "ctx", 0, 0, tiled=True, axis_index_groups=chips)
    keys = lax.all_to_all(
        jnp.broadcast_to(column[None], (HEADS,) + column.shape), "head", 0, 0, tiled=True
    )
    others = lax.ppermute(keys, "ctx", [(i, i ^ 1) for i in range(2 * CHIPS)])

    query = pl.pallas_call(
        query_kernel,
        out_shape=shape(HEADS * ROWS, WIDTH, dtype=BF16),
        in_specs=[VMEM] * 3,
        out_specs=VMEM,
        compiler_params=params(24),
        name="query",
    )(jnp.transpose(queries, (1, 0, 2)), absorb_k, table)

    state = (
        shape(HEADS * ROWS, 128),
        shape(HEADS * ROWS, 128),
        shape(HEADS * ROWS, LAT),
    )
    work = pl.CostEstimate(
        flops=2 * HEADS * ROWS * CHIPS * ROWS * (WIDTH + LAT),
        bytes_accessed=8 * MIB,
        transcendentals=HEADS * ROWS * CHIPS * ROWS,
    )
    state = pl.pallas_call(
        functools.partial(first_kernel, scale),
        out_shape=state,
        in_specs=[SMEM, VMEM, VMEM],
        out_specs=(VMEM,) * 3,
        compiler_params=params(32),
        cost_estimate=work,
        name="first",
    )(where, query, keys)
    flat, low = pl.pallas_call(
        functools.partial(second_kernel, scale),
        out_shape=(
            shape(ROWS, HEADS * VDIM, dtype=BF16),
            shape(3, ROWS, o_down.shape[1], dtype=BF16),
        ),
        in_specs=[SMEM] + [VMEM] * 7,
        out_specs=(VMEM,) * 2,
        scratch_shapes=[
            pltpu.VMEM((HEADS * ROWS, 128), F32),
            pltpu.VMEM((HEADS * ROWS, 128), F32),
            pltpu.VMEM((HEADS * ROWS, LAT), F32),
        ],
        compiler_params=params(32),
        cost_estimate=work,
        name="second",
    )(where, query, others, *state, absorb_v, o_down)

    terms = pl.pallas_call(
        output_kernel,
        grid=(out_cols // COLS,),
        out_shape=shape(out_cols, ROWS, dtype=BF16),
        in_specs=[
            pl.BlockSpec((ROWS, HEADS * VDIM), lambda i: (0, 0)),
            pl.BlockSpec((3, ROWS, o_up.shape[0]), lambda i: (0, 0, 0)),
            pl.BlockSpec((o_values.shape[0], COLS), lambda i: (0, i)),
            pl.BlockSpec((o_pattern.shape[0], COLS), lambda i: (0, i)),
            pl.BlockSpec((o_up.shape[0], COLS), lambda i: (0, i)),
        ],
        out_specs=pl.BlockSpec((COLS, ROWS), lambda i: (i, 0)),
        scratch_shapes=[pltpu.VMEM((2 * o_values.shape[0], COLS), BF16)],
        compiler_params=params(32),
        name="output",
    )(flat, low, o_values, o_pattern, o_up)
    shares = lax.all_to_all(
        terms.reshape(HEADS, out_cols // HEADS, ROWS), "head", 0, 0, tiled=True
    )
    return pl.pallas_call(
        sum_kernel,
        out_shape=shape(ROWS, out_cols // HEADS),
        in_specs=[VMEM],
        out_specs=VMEM,
        compiler_params=params(24),
        name="total",
    )(shares)


def solution(mesh):
    in_specs = (
        P("ctx", "head"),
        P("head", None),
        P("head", None),
        P("head", None),
        P(),
        P(),
        P("ctx", "head", None),
        P("head", None, None),
        P("head", None, None),
        P("head", None),
        P("head", None),
        P("head", None),
        P(),
    )
    out_specs = P("ctx", "head")
    return jax.shard_map(local, mesh=mesh, in_specs=in_specs, out_specs=out_specs, check_vma=False)
```

```python
import functools
import math

import jax
import jax.numpy as jnp
from jax import lax
from jax.experimental import pallas as pl
from jax.experimental.pallas import tpu as pltpu
from jax.sharding import PartitionSpec as P

BF16 = jnp.bfloat16
F32 = jnp.float32
MIB = 1024 * 1024
HEADS = 8
ROWS = 128
ALL = HEADS * ROWS
PIECE = ROWS // HEADS
LAT = 512
ROPE = 64
WIDTH = LAT + ROPE
NOPE = 128
VDIM = 128
CTX = 32
CHIPS = 8
GROUP = 4
KEYS = GROUP * ROWS
COLS = 640
LOG2E = 1.4426950408889634


def dot(a, b):
    return jnp.dot(a, b, preferred_element_type=F32)


def dot_first(a, b):
    return lax.dot_general(a, b, (((0,), (0,)), ((), ())), preferred_element_type=F32)


def dot_last(a, b):
    return lax.dot_general(a, b, (((1,), (1,)), ((), ())), preferred_element_type=F32)


def unpair(count):
    half = count // 2
    rows = lax.broadcasted_iota(jnp.int32, (count, count), 0)
    columns = lax.broadcasted_iota(jnp.int32, (count, count), 1)
    wanted = jnp.where(rows < half, 2 * rows, 2 * (rows - half) + 1)
    return jnp.where(columns == wanted, 1.0, 0.0).astype(BF16)


def by_slot():
    rows = lax.broadcasted_iota(jnp.int32, (128, 128), 0)
    columns = lax.broadcasted_iota(jnp.int32, (128, 128), 1)
    return jnp.where(rows == 4 * (columns % 32) + columns // 32, 1.0, 0.0).astype(BF16)


def densify(values_ref, pattern_ref, dense_ref):
    total = values_ref.shape[0]
    begin = 0
    while begin < total:
        count = min(256, total - begin)
        half = count // 2
        pair = dot(unpair(count), values_ref[begin : begin + count, :])
        v0, v1 = pair[:half], pair[half:]
        p = pattern_ref[begin // 2 : begin // 2 + half, :]
        slots = (
            jnp.where(p < 3, v0, 0.0),
            jnp.where(p == 0, v1, jnp.where((p == 3) | (p == 4), v0, 0.0)),
            jnp.where((p == 1) | (p == 3), v1, jnp.where(p == 5, v0, 0.0)),
            jnp.where((p == 2) | (p >= 4), v1, 0.0),
        )
        for k, slot in enumerate(slots):
            slot = slot.astype(BF16)
            for b in range(half // 32):
                row = 2 * begin + 128 * b + 32 * k
                dense_ref[row : row + 32, :] = slot[32 * b : 32 * b + 32]
        begin += count


def thirds(x):
    high = x.astype(BF16)
    rest = x - high.astype(F32)
    middle = rest.astype(BF16)
    low = (rest - middle.astype(F32)).astype(BF16)
    return high, middle, low


def project_kernel(
    tokens_hbm, values_hbm, pattern_hbm, down_hbm, up_hbm,
    raw_ref, tokens_ref, values_ref, pattern_ref, down_ref, up_ref, dense_ref, sems,
):
    copies = [
        pltpu.make_async_copy(source, target, sems.at[n])
        for n, (source, target) in enumerate(
            (
                (values_hbm, values_ref),
                (pattern_hbm, pattern_ref),
                (tokens_hbm, tokens_ref),
                (down_hbm, down_ref),
                (up_hbm, up_ref),
            )
        )
    ]
    for copy in copies:
        copy.start()
    for copy in copies:
        copy.wait()
    densify(values_ref, pattern_ref, dense_ref)
    order = by_slot()
    tokens = tokens_ref[...]
    parts = [dot(tokens[:, b : b + 128], order).astype(BF16) for b in range(0, tokens.shape[1], 128)]
    raw = dot(jnp.concatenate(parts, axis=1), dense_ref[...])
    up = up_ref[...]
    for term in thirds(dot_last(tokens, down_ref[...])):
        raw += dot(term, up)
    raw_ref[...] = raw.reshape(raw_ref.shape)


def query_kernel(queries_ref, absorb_ref, table_ref, out_ref):
    half = ROPE // 2
    cos, sin = table_ref[:ROPE, :], table_ref[ROPE:, :]
    for h in range(HEADS):
        columns = slice(h * ROWS, (h + 1) * ROWS)
        out_ref[:LAT, columns] = dot_first(absorb_ref[h], queries_ref[h, :NOPE, :]).astype(BF16)
        x = queries_ref[h, NOPE:, :].astype(F32)
        swapped = jnp.concatenate([x[half:], x[:half]], axis=0)
        out_ref[LAT:, columns] = (x * cos + swapped * sin).astype(BF16)


def finish_kernel(where_ref, parts_ref, gain_ref, table_ref, out_ref):
    raw = parts_ref[0]
    for h in range(1, HEADS):
        raw += parts_ref[h]
    latent = raw[:, :LAT]
    meansq = jnp.mean(latent * latent, axis=-1, keepdims=True)
    normed = (latent * lax.rsqrt(meansq + 1e-06) * gain_ref[...]).astype(BF16)
    table = table_ref[pl.ds(pl.multiple_of(where_ref[3] * PIECE, PIECE), PIECE), :]
    x = raw[:, LAT:]
    half = ROPE // 2
    swapped = jnp.concatenate([x[:, half:], x[:, :half]], axis=1)
    turned = (x * table[:, :ROPE] + swapped * table[:, ROPE:]).astype(BF16)
    for c in range(CHIPS):
        out_ref[c, :, :LAT] = normed
        out_ref[c, :, LAT:] = turned


class Rows:
    def __init__(self, where_ref, q_ref, m_ref, l_ref, acc_ref, scale):
        self.chip, self.core = where_ref[1], where_ref[2]
        self.q_ref, self.m_ref, self.l_ref, self.acc_ref = q_ref, m_ref, l_ref, acc_ref
        self.scale = scale

    def clear(self):
        self.m_ref[...] = jnp.full(self.m_ref.shape, -jnp.inf, F32)
        self.l_ref[...] = jnp.zeros(self.l_ref.shape, F32)
        self.acc_ref[...] = jnp.zeros(self.acc_ref.shape, F32)

    def chunk(self, keys_ref, j, key_core=None):
        keys = jnp.concatenate(
            [keys_ref[:, GROUP * j + b].reshape(ROWS, WIDTH) for b in range(GROUP)], axis=0
        )
        scores = dot(keys, self.q_ref[...]) * self.scale
        if key_core is not None:
            query = lax.broadcasted_iota(jnp.int32, (1, ALL), 1) % ROWS
            key = lax.broadcasted_iota(jnp.int32, (KEYS, 1), 0)
            ahead = (2 * self.chip + self.core) * ROWS + query
            place = (2 * (GROUP * j + key // ROWS) + key_core) * ROWS + key % ROWS
            scores = jnp.where(place <= ahead, scores, -jnp.inf)
        old = self.m_ref[...]
        new = jnp.maximum(old, jnp.max(scores, axis=0, keepdims=True))
        factor = jnp.exp2(old - new)
        weights = jnp.exp2(scores - new[:1])
        self.m_ref[...] = new
        self.l_ref[...] = self.l_ref[...] * factor + jnp.sum(
            weights.reshape(KEYS // 8, 8, ALL), axis=0
        )
        self.acc_ref[...] = self.acc_ref[...] * factor[:1] + dot(
            keys[:, :LAT].T, weights.astype(BF16)
        )

    def whole(self, keys_ref, count):
        @pl.loop(0, count)
        def _(j):
            self.chunk(keys_ref, j)

    def causal(self, keys_ref, key_core):
        self.whole(keys_ref, self.chip // GROUP)
        self.chunk(keys_ref, self.chip // GROUP, key_core)

    def head_out(self, h, absorb_ref):
        columns = slice(h * ROWS, (h + 1) * ROWS)
        total = jnp.sum(self.l_ref[:, columns], axis=0, keepdims=True)
        attended = (self.acc_ref[:, columns] / total).astype(BF16)
        return dot_first(absorb_ref[h], attended), self.m_ref[:1, columns] + jnp.log2(total)


def first_kernel(scale, where_ref, own_ref, partner_ref, keys_ref, m_ref, l_ref, acc_ref):
    upper = where_ref[0]
    for q_ref, mine in ((own_ref, upper == 1), (partner_ref, upper == 0)):
        rows = Rows(where_ref, q_ref, m_ref, l_ref, acc_ref, scale)

        @pl.when(mine)
        def _():
            rows.clear()
            if q_ref is own_ref:
                rows.causal(keys_ref, where_ref[2])
            else:
                rows.whole(keys_ref, CHIPS // GROUP)


def second_kernel(
    scale, where_ref, own_ref, partner_ref, keys_ref, absorb_ref, m_in, l_in, acc_in,
    part_ref, m_ref, l_ref, acc_ref,
):
    del m_in, l_in, acc_in
    upper = where_ref[0]

    @pl.when(upper == 1)
    def _():
        rows = Rows(where_ref, own_ref, m_ref, l_ref, acc_ref, scale)
        rows.causal(keys_ref, 1 - where_ref[2])

    @pl.when(upper == 0)
    def _():
        rows = Rows(where_ref, partner_ref, m_ref, l_ref, acc_ref, scale)
        rows.whole(keys_ref, CHIPS // GROUP)
        logs = []
        for h in range(HEADS):
            out, log = rows.head_out(h, absorb_ref)
            part_ref[h * VDIM : (h + 1) * VDIM, :] = out.astype(BF16)
            logs.append(log)
        logs = jnp.concatenate(logs, axis=0)
        terms = [t.astype(F32) for t in thirds(logs)] + [jnp.zeros_like(logs)]
        part_ref[HEADS * VDIM :, :] = jnp.concatenate(terms, axis=0).astype(BF16)


def third_kernel(
    scale, where_ref, own_ref, keys_ref, others_ref, m_in, l_in, acc_in, m_ref, l_ref, acc_ref
):
    del m_in, l_in, acc_in

    @pl.when(where_ref[0] == 0)
    def _():
        rows = Rows(where_ref, own_ref, m_ref, l_ref, acc_ref, scale)
        rows.clear()
        rows.causal(keys_ref, where_ref[2])
        rows.causal(others_ref, 1 - where_ref[2])


def output_kernel(
    where_ref, m_ref, l_ref, acc_ref, part_ref, absorb_ref, down_ref, up_ref, dense_ref,
    out_ref, flat_ref,
):
    upper = where_ref[0]
    rows = Rows(where_ref, None, m_ref, l_ref, acc_ref, None)
    logs = part_ref[HEADS * VDIM :, :].astype(F32)
    logs = logs[:HEADS] + logs[HEADS : 2 * HEADS] + logs[2 * HEADS : 3 * HEADS]
    order = by_slot()
    lowrank = jnp.zeros((down_ref.shape[0], ROWS), F32)
    for h in range(HEADS):
        span = slice(h * VDIM, (h + 1) * VDIM)
        mine, log = rows.head_out(h, absorb_ref)
        other_log = jnp.where(upper == 1, logs[h : h + 1], -jnp.inf)
        top = jnp.maximum(log, other_log)
        weight, other_weight = jnp.exp2(log - top), jnp.exp2(other_log - top)
        other = part_ref[span, :].astype(F32)
        out = (mine * weight + other * other_weight) / (weight + other_weight)
        out = out.astype(BF16)
        lowrank += dot(down_ref[:, span], out)
        flat_ref[span, :] = dot_first(order, out).astype(BF16)
    low = thirds(lowrank)
    for c in range(0, out_ref.shape[0], COLS):
        terms = dot_first(flat_ref[...], dense_ref[:, c : c + COLS])
        for term in low:
            terms += dot_first(term, up_ref[:, c : c + COLS])
        out_ref[c : c + COLS, :] = terms.T.astype(BF16)


def sum_kernel(parts_ref, out_ref):
    total = parts_ref[0].astype(F32)
    for h in range(1, HEADS):
        total += parts_ref[h].astype(F32)
    out_ref[...] = total


def shape(*dims, dtype=F32):
    return jax.ShapeDtypeStruct(dims, dtype)


def params(mib):
    return pltpu.CompilerParams(vmem_limit_bytes=mib * MIB)


def cost(flops, nbytes, exps=0):
    return pl.CostEstimate(flops=flops, bytes_accessed=nbytes, transcendentals=exps)


VMEM = pl.BlockSpec(memory_space=pltpu.VMEM)
SMEM = pl.BlockSpec(memory_space=pltpu.SMEM)
ANY = pl.BlockSpec(memory_space=pl.ANY)


def tables(positions):
    half = ROPE // 2
    freqs = 10000.0 ** (-jnp.arange(half, dtype=F32) / half)
    angles = positions.astype(F32)[:, None] * freqs
    cos, sin = jnp.cos(angles), jnp.sin(angles)
    return jnp.concatenate([cos, cos, -sin, sin], axis=1)


def local(
    tokens, kv_values, kv_pattern, kv_down, kv_up, kv_gain, queries, absorb_k, absorb_v,
    o_values, o_pattern, o_down, o_up,
):
    ctx = lax.axis_index("ctx")
    head = lax.axis_index("head")
    upper = ctx // (2 * CHIPS)
    where = jnp.stack([upper, (ctx // 2) % CHIPS, ctx % 2, head]).astype(jnp.int32)
    scale = LOG2E / math.sqrt(queries.shape[2])
    out_cols = o_values.shape[1]
    rank = o_down.shape[1]

    columns = jnp.transpose(queries, (1, 2, 0))
    partner = lax.ppermute(columns, "ctx", [(i + 2 * CHIPS, i) for i in range(2 * CHIPS)])

    raw = pl.pallas_call(
        project_kernel,
        out_shape=shape(HEADS, PIECE, WIDTH),
        in_specs=[ANY] * 5,
        out_specs=VMEM,
        scratch_shapes=[
            pltpu.VMEM(tokens.shape, BF16),
            pltpu.VMEM(kv_values.shape, BF16),
            pltpu.VMEM(kv_pattern.shape, jnp.int32),
            pltpu.VMEM(kv_down.shape[::-1], BF16),
            pltpu.VMEM(kv_up.shape, BF16),
            pltpu.VMEM((tokens.shape[1], WIDTH), BF16),
            pltpu.SemaphoreType.DMA((5,)),
        ],
        compiler_params=params(24),
        name="project",
    )(tokens, kv_values, kv_pattern, kv_down.T, kv_up)
    parts = lax.all_to_all(raw, "head", 0, 0, tiled=True)

    positions = ctx * ROWS + jnp.arange(ROWS, dtype=jnp.int32)
    table = tables(positions)
    partner_table = tables(positions + 2 * CHIPS * ROWS)

    piece = pl.pallas_call(
        finish_kernel,
        out_shape=shape(CHIPS, PIECE, WIDTH, dtype=BF16),
        in_specs=[SMEM, VMEM, VMEM, VMEM],
        out_specs=VMEM,
        compiler_params=params(16),
        name="finish",
    )(where, parts, kv_gain.reshape(1, LAT), table)

    along_z = [
        [(u * CHIPS + chip) * 2 + core for chip in range(CHIPS)]
        for u in range(2)
        for core in range(2)
    ]
    column = lax.all_to_all(piece, "ctx", 0, 0, tiled=True, axis_index_groups=along_z)
    keys = lax.all_to_all(
        jnp.broadcast_to(column[None], (HEADS,) + column.shape), "head", 0, 0, tiled=True
    )
    others = lax.ppermute(keys, "ctx", [(i, i ^ 1) for i in range(CTX)])

    def query(x, t):
        return pl.pallas_call(
            query_kernel,
            out_shape=shape(WIDTH, ALL, dtype=BF16),
            in_specs=[VMEM] * 3,
            out_specs=VMEM,
            compiler_params=params(16),
            cost_estimate=cost(2 * ALL * NOPE * LAT, 4 * MIB),
            name="query",
        )(x, absorb_k, t.T)

    own_query = query(columns, table)
    partner_query = query(partner, partner_table)

    dense = pl.pallas_call(
        densify,
        grid=(out_cols // COLS,),
        out_shape=shape(2 * o_values.shape[0], out_cols, dtype=BF16),
        in_specs=[
            pl.BlockSpec((o_values.shape[0], COLS), lambda i: (0, i)),
            pl.BlockSpec((o_pattern.shape[0], COLS), lambda i: (0, i)),
        ],
        out_specs=pl.BlockSpec((2 * o_values.shape[0], COLS), lambda i: (0, i)),
        compiler_params=params(24),
        cost_estimate=cost(2 * 256 * o_values.size, 12 * MIB),
        name="densify",
    )(o_values, o_pattern)

    state = (shape(8, ALL), shape(8, ALL), shape(LAT, ALL))
    scores = ALL * CHIPS * ROWS
    work = cost(2 * scores * (WIDTH + LAT), 8 * MIB, scores)
    first = pl.pallas_call(
        functools.partial(first_kernel, scale),
        out_shape=state,
        in_specs=[SMEM, VMEM, VMEM, VMEM],
        out_specs=(VMEM,) * 3,
        compiler_params=params(32),
        cost_estimate=work,
        name="first",
    )(where, own_query, partner_query, keys)
    part, *second = pl.pallas_call(
        functools.partial(second_kernel, scale),
        out_shape=(shape(HEADS * VDIM + 4 * HEADS, ROWS, dtype=BF16),) + state,
        in_specs=[SMEM] + [VMEM] * 7,
        out_specs=(VMEM,) * 4,
        input_output_aliases={5: 1, 6: 2, 7: 3},
        compiler_params=params(32),
        cost_estimate=work,
        name="second",
    )(where, own_query, partner_query, others, absorb_v, *first)
    received = lax.ppermute(part, "ctx", [(i, i + 2 * CHIPS) for i in range(2 * CHIPS)])
    third = pl.pallas_call(
        functools.partial(third_kernel, scale),
        out_shape=state,
        in_specs=[SMEM] + [VMEM] * 6,
        out_specs=(VMEM,) * 3,
        input_output_aliases={4: 0, 5: 1, 6: 2},
        compiler_params=params(32),
        cost_estimate=work,
        name="third",
    )(where, own_query, keys, others, *second)

    terms = pl.pallas_call(
        output_kernel,
        out_shape=shape(out_cols, ROWS, dtype=BF16),
        in_specs=[SMEM] + [VMEM] * 8,
        out_specs=VMEM,
        scratch_shapes=[pltpu.VMEM((HEADS * VDIM, ROWS), BF16)],
        compiler_params=params(32),
        cost_estimate=cost(2 * ROWS * HEADS * VDIM * out_cols, 8 * MIB),
        name="output",
    )(where, *third, received, absorb_v, o_down.T, o_up, dense)
    shares = lax.all_to_all(
        terms.reshape(HEADS, out_cols // HEADS, ROWS), "head", 0, 0, tiled=True
    )
    return pl.pallas_call(
        sum_kernel,
        out_shape=shape(out_cols // HEADS, ROWS),
        in_specs=[VMEM],
        out_specs=VMEM,
        compiler_params=params(16),
        name="total",
    )(shares).T


def solution(mesh):
    in_specs = (
        P("ctx", "head"),
        P("head", None),
        P("head", None),
        P("head", None),
        P(),
        P(),
        P("ctx", "head", None),
        P("head", None, None),
        P("head", None, None),
        P("head", None),
        P("head", None),
        P("head", None),
        P(),
    )
    out_specs = P("ctx", "head")
    return jax.shard_map(local, mesh=mesh, in_specs=in_specs, out_specs=out_specs, check_vma=False)
```

```python
import functools
import math

import jax
import jax.numpy as jnp
from jax import lax
from jax.experimental import pallas as pl
from jax.experimental.pallas import tpu as pltpu
from jax.sharding import PartitionSpec as P

BF16 = jnp.bfloat16
F32 = jnp.float32
MIB = 1024 * 1024
HEADS = 8
ROWS = 128
ALL = HEADS * ROWS
PIECE = ROWS // HEADS
LAT = 512
ROPE = 64
WIDTH = LAT + ROPE
NOPE = 128
VDIM = 128
CTX = 32
CHIPS = 8
SLICES = 4
PACKED = ROWS * WIDTH // 128
KEYS = SLICES * ROWS
WIDE = 640
UNSEEN = -1e30
COLS = 640
LOG2E = 1.4426950408889634


def dot(a, b):
    return jnp.dot(a, b, preferred_element_type=F32)


def dot_first(a, b):
    return lax.dot_general(a, b, (((0,), (0,)), ((), ())), preferred_element_type=F32)


def dot_last(a, b):
    return lax.dot_general(a, b, (((1,), (1,)), ((), ())), preferred_element_type=F32)


def unpair(count):
    half = count // 2
    rows = lax.broadcasted_iota(jnp.int32, (count, count), 0)
    columns = lax.broadcasted_iota(jnp.int32, (count, count), 1)
    wanted = jnp.where(rows < half, 2 * rows, 2 * (rows - half) + 1)
    return jnp.where(columns == wanted, 1.0, 0.0).astype(BF16)


def by_slot():
    rows = lax.broadcasted_iota(jnp.int32, (128, 128), 0)
    columns = lax.broadcasted_iota(jnp.int32, (128, 128), 1)
    return jnp.where(rows == 4 * (columns % 32) + columns // 32, 1.0, 0.0).astype(BF16)


def densify(values_ref, pattern_ref, dense_ref):
    total = values_ref.shape[0]
    zero = jnp.zeros((), BF16)
    begin = 0
    while begin < total:
        count = min(256, total - begin)
        half = count // 2
        pair = dot(unpair(count), values_ref[begin : begin + count, :]).astype(BF16)
        v0, v1 = pair[:half], pair[half:]
        p = pattern_ref[begin // 2 : begin // 2 + half, :].astype(F32).astype(BF16)
        is_0, is_1, is_2, is_3, is_4, is_5 = (p == jnp.asarray(k, BF16) for k in range(6))
        slots = (
            jnp.where(p < jnp.asarray(3, BF16), v0, zero),
            jnp.where(is_0, v1, jnp.where(is_3 | is_4, v0, zero)),
            jnp.where(is_1 | is_3, v1, jnp.where(is_5, v0, zero)),
            jnp.where(is_2 | is_4 | is_5, v1, zero),
        )
        for k, slot in enumerate(slots):
            for b in range(half // 32):
                row = 2 * begin + 128 * b + 32 * k
                dense_ref[row : row + 32, :] = slot[32 * b : 32 * b + 32]
        begin += count


def thirds(x):
    high = x.astype(BF16)
    rest = x - high.astype(F32)
    middle = rest.astype(BF16)
    low = (rest - middle.astype(F32)).astype(BF16)
    return high, middle, low


def project_kernel(
    tokens_hbm, values_hbm, pattern_hbm, down_hbm, up_hbm,
    raw_ref, tokens_ref, values_ref, pattern_ref, down_ref, up_ref, dense_ref, sems,
):
    copies = [
        pltpu.make_async_copy(source, target, sems.at[n])
        for n, (source, target) in enumerate(
            (
                (values_hbm, values_ref),
                (pattern_hbm, pattern_ref),
                (tokens_hbm, tokens_ref),
                (down_hbm, down_ref),
                (up_hbm, up_ref),
            )
        )
    ]
    for copy in copies:
        copy.start()
    for copy in copies:
        copy.wait()
    densify(values_ref, pattern_ref, dense_ref)
    order = by_slot()
    tokens = tokens_ref[...]
    parts = [dot(tokens[:, b : b + 128], order).astype(BF16) for b in range(0, tokens.shape[1], 128)]
    raw = dot(jnp.concatenate(parts, axis=1), dense_ref[...])
    up = up_ref[...]
    for term in thirds(dot_last(tokens, down_ref[...])):
        raw += dot(term, up)
    raw_ref[:, :, :WIDTH] = raw.reshape(HEADS, PIECE, WIDTH)
    raw_ref[:, :, WIDTH:] = jnp.zeros((HEADS, PIECE, WIDE - WIDTH), F32)


def query_kernel(queries_ref, absorb_ref, table_ref, out_ref, token_ref):
    token_ref[...] = jnp.zeros(token_ref.shape, F32)
    half = ROPE // 2
    cos, sin = table_ref[:ROPE, :], table_ref[ROPE:, :]
    for h in range(HEADS):
        columns = slice(h * ROWS, (h + 1) * ROWS)
        out_ref[:LAT, columns] = dot_first(absorb_ref[h], queries_ref[h, :NOPE, :]).astype(BF16)
        x = queries_ref[h, NOPE:, :].astype(F32)
        swapped = jnp.concatenate([x[half:], x[:half]], axis=0)
        out_ref[LAT:, columns] = (x * cos + swapped * sin).astype(BF16)


def finish_kernel(where_ref, parts_ref, gain_ref, table_ref, *refs):
    out_ref = refs[-1]
    raw = parts_ref[0]
    for h in range(1, HEADS):
        raw += parts_ref[h]
    latent = raw[:, :LAT]
    meansq = jnp.mean(latent * latent, axis=-1, keepdims=True)
    normed = (latent * lax.rsqrt(meansq + 1e-06) * gain_ref[...]).astype(BF16)
    table = table_ref[pl.ds(pl.multiple_of(where_ref[3] * PIECE, PIECE), PIECE), :]
    x = raw[:, LAT:WIDTH]
    half = ROPE // 2
    swapped = jnp.concatenate([x[:, half:], x[:, :half]], axis=1)
    turned = (x * table[:, :ROPE] + swapped * table[:, ROPE:]).astype(BF16)
    for c in range(CHIPS):
        out_ref[c, :, :LAT] = normed
        out_ref[c, :, LAT:WIDTH] = turned
        out_ref[c, :, WIDTH:] = jnp.zeros((PIECE, WIDE - WIDTH), BF16)


def pack_kernel(column_ref, *refs):
    out_ref = refs[-1]
    keys = column_ref[...].reshape(ROWS, WIDE)
    rope = keys[:, LAT:WIDTH]
    rope = jnp.concatenate([rope[: ROWS // 2], rope[ROWS // 2 :]], axis=1)
    for k in range(HEADS):
        for c in range(LAT // 128):
            out_ref[k, c * ROWS : (c + 1) * ROWS, :] = keys[:, c * 128 : (c + 1) * 128]
        out_ref[k, LAT // 128 * ROWS :, :] = rope


def unpack(keys_ref, part):
    latents, ropes = [], []
    for k in range(part * SLICES, (part + 1) * SLICES):
        latents.append(
            jnp.concatenate(
                [keys_ref[k, c * ROWS : (c + 1) * ROWS, :] for c in range(LAT // 128)], axis=1
            )
        )
        rope = keys_ref[k, LAT // 128 * ROWS :, :]
        ropes += [rope[:, :ROPE], rope[:, ROPE:]]
    return jnp.concatenate(latents, axis=0), jnp.concatenate(ropes, axis=0)


class Rows:
    def __init__(self, where_ref, q_ref, m_ref, l_ref, acc_ref, scale):
        self.chip, self.core = where_ref[1], where_ref[2]
        self.q_ref, self.m_ref, self.l_ref, self.acc_ref = q_ref, m_ref, l_ref, acc_ref
        self.scale = scale

    def clear(self):
        self.m_ref[...] = jnp.full(self.m_ref.shape, UNSEEN, F32)
        self.l_ref[...] = jnp.zeros(self.l_ref.shape, F32)
        self.acc_ref[...] = jnp.zeros(self.acc_ref.shape, F32)

    def chunk(self, keys_ref, part, key_core=None):
        latent, rope = unpack(keys_ref, part)
        scores = dot(jnp.concatenate([latent, rope], axis=1), self.q_ref[...]) * self.scale
        if key_core is not None:
            query = lax.broadcasted_iota(jnp.int32, (1, ALL), 1) % ROWS
            key = lax.broadcasted_iota(jnp.int32, (KEYS, 1), 0)
            ahead = (2 * self.chip + self.core) * ROWS + query
            place = (2 * (key % ROWS // PIECE) + key_core) * ROWS
            place += (part * SLICES + key // ROWS) * PIECE + key % PIECE
            scores = jnp.where(place <= ahead, scores, UNSEEN)
        old = self.m_ref[...]
        new = jnp.maximum(old, jnp.max(scores, axis=0, keepdims=True))
        factor = jnp.exp2(old - new)
        weights = jnp.exp2(scores - new[:1])
        self.m_ref[...] = new
        self.l_ref[...] = self.l_ref[...] * factor + jnp.sum(
            weights.reshape(KEYS // 8, 8, ALL), axis=0
        )
        self.acc_ref[...] = self.acc_ref[...] * factor[:1] + dot(latent.T, weights.astype(BF16))

    def run(self, keys_ref, key_core=None):
        for part in range(HEADS // SLICES):
            self.chunk(keys_ref, part, key_core)

    def head_out(self, h, absorb_ref):
        columns = slice(h * ROWS, (h + 1) * ROWS)
        total = jnp.sum(self.l_ref[:, columns], axis=0, keepdims=True)
        attended = (self.acc_ref[:, columns] * (1.0 / total)).astype(BF16)
        return dot_first(absorb_ref[h], attended), self.m_ref[:1, columns] + jnp.log2(total)


def first_kernel(scale, where_ref, own_ref, partner_ref, keys_ref, *state):
    @pl.when(where_ref[0] == 0)
    def _():
        rows = Rows(where_ref, partner_ref, *state, scale)
        rows.clear()
        rows.run(keys_ref)

    @pl.when(where_ref[0] == 1)
    def _():
        rows = Rows(where_ref, own_ref, *state, scale)
        rows.clear()
        rows.run(keys_ref, where_ref[2])


def second_kernel(scale, where_ref, own_ref, partner_ref, keys_ref, absorb_ref, *refs):
    part_ref, *state = refs[3:]

    @pl.when(where_ref[0] == 0)
    def _():
        rows = Rows(where_ref, partner_ref, *state, scale)
        rows.run(keys_ref)
        outs = [rows.head_out(h, absorb_ref) for h in range(HEADS)]
        for h, (out, _) in enumerate(outs):
            part_ref[h * VDIM : (h + 1) * VDIM, :] = out.astype(BF16)
        logs = jnp.concatenate([log for _, log in outs], axis=0)
        terms = [t.astype(F32) for t in thirds(logs)] + [jnp.zeros_like(logs)]
        part_ref[HEADS * VDIM :, :] = jnp.concatenate(terms, axis=0).astype(BF16)

    @pl.when(where_ref[0] == 1)
    def _():
        Rows(where_ref, own_ref, *state, scale).run(keys_ref, 1 - where_ref[2])


def third_kernel(scale, where_ref, own_ref, keys_ref, others_ref, *refs):
    @pl.when(where_ref[0] == 0)
    def _():
        rows = Rows(where_ref, own_ref, *refs[3:], scale)
        rows.clear()
        rows.run(keys_ref, where_ref[2])
        rows.run(others_ref, 1 - where_ref[2])


def output_kernel(
    where_ref, m_ref, l_ref, acc_ref, part_ref, absorb_ref, down_ref, up_ref, dense_ref,
    out_ref,
):
    upper = where_ref[0]
    rows = Rows(where_ref, None, m_ref, l_ref, acc_ref, None)
    logs = part_ref[HEADS * VDIM :, :].astype(F32)
    logs = logs[:HEADS] + logs[HEADS : 2 * HEADS] + logs[2 * HEADS : 3 * HEADS]
    mine = [rows.head_out(h, absorb_ref) for h in range(HEADS)]
    outs = []
    for h, (own, log) in enumerate(mine):
        other_log = jnp.where(upper == 1, logs[h : h + 1], -jnp.inf)
        top = jnp.maximum(log, other_log)
        weight, other_weight = jnp.exp2(log - top), jnp.exp2(other_log - top)
        share = 1.0 / (weight + other_weight)
        other = part_ref[h * VDIM : (h + 1) * VDIM, :].astype(F32)
        outs.append((own * (weight * share) + other * (other_weight * share)).astype(BF16))
    order = by_slot()
    flat = jnp.concatenate([dot_first(out, order).astype(BF16) for out in outs], axis=1)
    lowrank = dot(down_ref[...], jnp.concatenate(outs, axis=0))
    low = jnp.concatenate(thirds(lowrank.T), axis=1)
    for c in range(0, out_ref.shape[0], COLS):
        up = up_ref[:, c : c + COLS]
        terms = dot(flat, dense_ref[:, c : c + COLS])
        terms += dot(low, jnp.concatenate([up] * 3, axis=0))
        out_ref[c : c + COLS, :] = terms.T.astype(BF16)


def sum_kernel(parts_ref, out_ref):
    total = parts_ref[0].astype(F32)
    for h in range(1, HEADS):
        total += parts_ref[h].astype(F32)
    out_ref[...] = total


def shape(*dims, dtype=F32):
    return jax.ShapeDtypeStruct(dims, dtype)


def params(mib):
    return pltpu.CompilerParams(vmem_limit_bytes=mib * MIB)


def cost(flops, nbytes, exps=0):
    return pl.CostEstimate(flops=flops, bytes_accessed=nbytes, transcendentals=exps)


VMEM = pl.BlockSpec(memory_space=pltpu.VMEM)
SMEM = pl.BlockSpec(memory_space=pltpu.SMEM)
ANY = pl.BlockSpec(memory_space=pl.ANY)


def tables(positions):
    half = ROPE // 2
    freqs = 10000.0 ** (-jnp.arange(half, dtype=F32) / half)
    angles = positions.astype(F32)[:, None] * freqs
    cos, sin = jnp.cos(angles), jnp.sin(angles)
    return jnp.concatenate([cos, cos, -sin, sin], axis=1)


def local(
    tokens, kv_values, kv_pattern, kv_down, kv_up, kv_gain, queries, absorb_k, absorb_v,
    o_values, o_pattern, o_down, o_up,
):
    ctx = lax.axis_index("ctx")
    head = lax.axis_index("head")
    upper = ctx // (2 * CHIPS)
    where = jnp.stack([upper, (ctx // 2) % CHIPS, ctx % 2, head]).astype(jnp.int32)
    scale = LOG2E / math.sqrt(queries.shape[2])
    out_cols = o_values.shape[1]
    rank = o_down.shape[1]

    columns = jnp.transpose(queries, (1, 2, 0))
    partner = lax.ppermute(columns, "ctx", [(i + 2 * CHIPS, i) for i in range(2 * CHIPS)])

    raw = pl.pallas_call(
        project_kernel,
        out_shape=shape(HEADS, PIECE, WIDE),
        in_specs=[ANY] * 5,
        out_specs=VMEM,
        scratch_shapes=[
            pltpu.VMEM(tokens.shape, BF16),
            pltpu.VMEM(kv_values.shape, BF16),
            pltpu.VMEM(kv_pattern.shape, jnp.int32),
            pltpu.VMEM(kv_down.shape[::-1], BF16),
            pltpu.VMEM(kv_up.shape, BF16),
            pltpu.VMEM((tokens.shape[1], WIDTH), BF16),
            pltpu.SemaphoreType.DMA((5,)),
        ],
        compiler_params=params(56),
        name="project",
    )(tokens, kv_values, kv_pattern, kv_down.T, kv_up)
    parts = lax.all_to_all(raw, "head", 0, 0, tiled=True)

    positions = ctx * ROWS + jnp.arange(ROWS, dtype=jnp.int32)
    table = tables(positions)
    partner_table = tables(positions + 2 * CHIPS * ROWS)

    def query(x, t):
        return pl.pallas_call(
            query_kernel,
            out_shape=(shape(WIDTH, ALL, dtype=BF16), shape(8, 128)),
            in_specs=[VMEM] * 3,
            out_specs=(VMEM, VMEM),
            compiler_params=params(16),
            cost_estimate=cost(2 * ALL * NOPE * LAT, 4 * MIB),
            name="query",
        )(x, absorb_k, t.T)

    own_query, own_token = query(columns, table)
    partner_query, partner_token = query(partner, partner_table)

    step = out_cols // 2
    dense = pl.pallas_call(
        densify,
        grid=(out_cols // step,),
        out_shape=shape(2 * o_values.shape[0], out_cols, dtype=BF16),
        in_specs=[
            pl.BlockSpec((o_values.shape[0], step), lambda i: (0, i)),
            pl.BlockSpec((o_pattern.shape[0], step), lambda i: (0, i)),
        ],
        out_specs=pl.BlockSpec((2 * o_values.shape[0], step), lambda i: (0, i)),
        compiler_params=params(24),
        cost_estimate=cost(2 * 256 * o_values.size, 12 * MIB),
        name="densify",
    )(o_values, o_pattern)

    piece = pl.pallas_call(
        finish_kernel,
        out_shape=shape(CHIPS, PIECE, WIDE, dtype=BF16),
        in_specs=[SMEM] + [VMEM] * 4,
        out_specs=VMEM,
        compiler_params=params(16),
        name="finish",
    )(where, parts, kv_gain.reshape(1, LAT), table, own_token)

    along_z = [
        [(u * CHIPS + chip) * 2 + core for chip in range(CHIPS)]
        for u in range(2)
        for core in range(2)
    ]
    column = lax.all_to_all(piece, "ctx", 0, 0, tiled=True, axis_index_groups=along_z)
    packed = pl.pallas_call(
        pack_kernel,
        out_shape=shape(HEADS, PACKED, 128, dtype=BF16),
        in_specs=[VMEM] * 2,
        out_specs=VMEM,
        compiler_params=params(16),
        name="pack",
    )(column, partner_token)
    keys = lax.all_to_all(packed, "head", 0, 0, tiled=True)
    others = lax.ppermute(keys, "ctx", [(i, i ^ 1) for i in range(CTX)])

    state = (shape(8, ALL), shape(8, ALL), shape(LAT, ALL))
    scores = ALL * CHIPS * ROWS
    work = cost(2 * scores * (WIDTH + LAT), 8 * MIB, scores)
    first = pl.pallas_call(
        functools.partial(first_kernel, scale),
        out_shape=state,
        in_specs=[SMEM, VMEM, VMEM, VMEM],
        out_specs=(VMEM,) * 3,
        compiler_params=params(32),
        cost_estimate=work,
        name="first",
    )(where, own_query, partner_query, keys)
    part, *second = pl.pallas_call(
        functools.partial(second_kernel, scale),
        out_shape=(shape(HEADS * VDIM + 4 * HEADS, ROWS, dtype=BF16),) + state,
        in_specs=[SMEM] + [VMEM] * 7,
        out_specs=(VMEM,) * 4,
        input_output_aliases={5: 1, 6: 2, 7: 3},
        compiler_params=params(32),
        cost_estimate=work,
        name="second",
    )(where, own_query, partner_query, others, absorb_v, *first)
    received = lax.ppermute(part, "ctx", [(i, i + 2 * CHIPS) for i in range(2 * CHIPS)])
    own = pl.pallas_call(
        functools.partial(third_kernel, scale),
        out_shape=state,
        in_specs=[SMEM] + [VMEM] * 6,
        out_specs=(VMEM,) * 3,
        input_output_aliases={4: 0, 5: 1, 6: 2},
        compiler_params=params(32),
        cost_estimate=work,
        name="third",
    )(where, own_query, keys, others, *second)

    terms = pl.pallas_call(
        output_kernel,
        out_shape=shape(out_cols, ROWS, dtype=BF16),
        in_specs=[SMEM] + [VMEM] * 8,
        out_specs=VMEM,
        compiler_params=params(32),
        cost_estimate=cost(2 * ROWS * HEADS * VDIM * out_cols, 8 * MIB),
        name="output",
    )(where, *own, received, absorb_v, o_down.T, o_up, dense)
    shares = lax.all_to_all(
        terms.reshape(HEADS, out_cols // HEADS, ROWS), "head", 0, 0, tiled=True
    )
    return pl.pallas_call(
        sum_kernel,
        out_shape=shape(out_cols // HEADS, ROWS),
        in_specs=[VMEM],
        out_specs=VMEM,
        compiler_params=params(16),
        name="total",
    )(shares).T


def solution(mesh):
    in_specs = (
        P("ctx", "head"),
        P("head", None),
        P("head", None),
        P("head", None),
        P(),
        P(),
        P("ctx", "head", None),
        P("head", None, None),
        P("head", None, None),
        P("head", None),
        P("head", None),
        P("head", None),
        P(),
    )
    out_specs = P("ctx", "head")
    return jax.shard_map(local, mesh=mesh, in_specs=in_specs, out_specs=out_specs, check_vma=False)
```

```python
import functools
import math

import jax
import jax.numpy as jnp
from jax import lax
from jax.experimental import pallas as pl
from jax.experimental.pallas import tpu as pltpu
from jax.sharding import PartitionSpec as P

BF16 = jnp.bfloat16
F32 = jnp.float32
MIB = 1024 * 1024
HEADS = 8
ROWS = 128
ALL = HEADS * ROWS
PIECE = ROWS // HEADS
LAT = 512
ROPE = 64
WIDTH = LAT + ROPE
NOPE = 128
VDIM = 128
CTX = 32
CHIPS = 8
PACKED = ROWS * WIDTH // 128
HALF = ROWS // 2
KEYS = HEADS * HALF
WIDE = 640
UNSEEN = -1e30
COLS = 640
LOG2E = 1.4426950408889634


def dot(a, b):
    return jnp.dot(a, b, preferred_element_type=F32)


def dot_first(a, b):
    return lax.dot_general(a, b, (((0,), (0,)), ((), ())), preferred_element_type=F32)


def dot_last(a, b):
    return lax.dot_general(a, b, (((1,), (1,)), ((), ())), preferred_element_type=F32)


def unpair(count):
    half = count // 2
    rows = lax.broadcasted_iota(jnp.int32, (count, count), 0)
    columns = lax.broadcasted_iota(jnp.int32, (count, count), 1)
    wanted = jnp.where(rows < half, 2 * rows, 2 * (rows - half) + 1)
    return jnp.where(columns == wanted, 1.0, 0.0).astype(BF16)


def by_slot():
    rows = lax.broadcasted_iota(jnp.int32, (128, 128), 0)
    columns = lax.broadcasted_iota(jnp.int32, (128, 128), 1)
    return jnp.where(rows == 4 * (columns % 32) + columns // 32, 1.0, 0.0).astype(BF16)


def densify(values_ref, pattern_ref, dense_ref):
    total = values_ref.shape[0]
    zero = jnp.zeros((), BF16)
    begin = 0
    while begin < total:
        count = min(256, total - begin)
        half = count // 2
        pair = dot(unpair(count), values_ref[begin : begin + count, :]).astype(BF16)
        v0, v1 = pair[:half], pair[half:]
        p = pattern_ref[begin // 2 : begin // 2 + half, :].astype(F32).astype(BF16)
        is_0, is_1, is_2, is_3, is_4, is_5 = (p == jnp.asarray(k, BF16) for k in range(6))
        slots = (
            jnp.where(p < jnp.asarray(3, BF16), v0, zero),
            jnp.where(is_0, v1, jnp.where(is_3 | is_4, v0, zero)),
            jnp.where(is_1 | is_3, v1, jnp.where(is_5, v0, zero)),
            jnp.where(is_2 | is_4 | is_5, v1, zero),
        )
        for k, slot in enumerate(slots):
            for b in range(half // 32):
                row = 2 * begin + 128 * b + 32 * k
                dense_ref[row : row + 32, :] = slot[32 * b : 32 * b + 32]
        begin += count


def thirds(x):
    high = x.astype(BF16)
    rest = x - high.astype(F32)
    middle = rest.astype(BF16)
    low = (rest - middle.astype(F32)).astype(BF16)
    return high, middle, low


def project_kernel(
    tokens_hbm, values_hbm, pattern_hbm, down_hbm, up_hbm,
    raw_ref, tokens_ref, values_ref, pattern_ref, down_ref, up_ref, dense_ref, sems,
):
    copies = [
        pltpu.make_async_copy(source, target, sems.at[n])
        for n, (source, target) in enumerate(
            (
                (tokens_hbm, tokens_ref),
                (down_hbm, down_ref),
                (up_hbm, up_ref),
                (values_hbm, values_ref),
                (pattern_hbm, pattern_ref),
            )
        )
    ]
    for copy in copies:
        copy.start()
    for copy in copies[:3]:
        copy.wait()
    order = by_slot()
    tokens = tokens_ref[...]
    parts = [dot(tokens[:, b : b + 128], order).astype(BF16) for b in range(0, tokens.shape[1], 128)]
    low = jnp.concatenate(thirds(dot_last(tokens, down_ref[...])), axis=1)
    raw = dot(low, jnp.concatenate([up_ref[...]] * 3, axis=0))
    for copy in copies[3:]:
        copy.wait()
    densify(values_ref, pattern_ref, dense_ref)
    raw += dot(jnp.concatenate(parts, axis=1), dense_ref[...])
    for h in range(HEADS):
        piece = raw[h * PIECE : (h + 1) * PIECE]
        for c in range(LAT // 128):
            raw_ref[h, c * PIECE : (c + 1) * PIECE, :] = piece[:, c * 128 : (c + 1) * 128]
        rope = piece[:, LAT:]
        raw_ref[h, LAT // 128 * PIECE :, :] = jnp.concatenate(
            [rope[: PIECE // 2], rope[PIECE // 2 :]], axis=1
        )


def query_kernel(queries_ref, absorb_ref, table_ref, out_ref, token_ref):
    token_ref[...] = jnp.zeros(token_ref.shape, F32)
    half = ROPE // 2
    cos, sin = table_ref[:ROPE, :], table_ref[ROPE:, :]
    for h in range(HEADS):
        columns = slice(h * ROWS, (h + 1) * ROWS)
        out_ref[:LAT, columns] = dot_first(absorb_ref[h], queries_ref[h, :NOPE, :]).astype(BF16)
        x = queries_ref[h, NOPE:, :].astype(F32)
        swapped = jnp.concatenate([x[half:], x[:half]], axis=0)
        out_ref[LAT:, columns] = (x * cos + swapped * sin).astype(BF16)


def finish_kernel(where_ref, parts_ref, gain_ref, table_ref, *refs):
    out_ref = refs[-1]
    raw = parts_ref[0]
    for h in range(1, HEADS):
        raw += parts_ref[h]
    latent = jnp.concatenate(
        [raw[c * PIECE : (c + 1) * PIECE] for c in range(LAT // 128)], axis=1
    )
    rope = raw[LAT // 128 * PIECE :]
    meansq = jnp.mean(latent * latent, axis=-1, keepdims=True)
    normed = (latent * lax.rsqrt(meansq + 1e-06) * gain_ref[...]).astype(BF16)
    table = table_ref[pl.ds(pl.multiple_of(where_ref[3] * PIECE, PIECE), PIECE), :]
    x = jnp.concatenate([rope[:, :ROPE], rope[:, ROPE:]], axis=0)
    half = ROPE // 2
    swapped = jnp.concatenate([x[:, half:], x[:, :half]], axis=1)
    turned = (x * table[:, :ROPE] + swapped * table[:, ROPE:]).astype(BF16)
    for c in range(CHIPS):
        out_ref[c, :, :LAT] = normed
        out_ref[c, :, LAT:WIDTH] = turned
        out_ref[c, :, WIDTH:] = jnp.zeros((PIECE, WIDE - WIDTH), BF16)


def pack_kernel(column_ref, *refs):
    out_ref = refs[-1]
    keys = column_ref[...].reshape(ROWS, WIDE)
    rope = keys[:, LAT:WIDTH]
    rope = jnp.concatenate([rope[: ROWS // 2], rope[ROWS // 2 :]], axis=1)
    for k in range(HEADS):
        for c in range(LAT // 128):
            out_ref[k, c * ROWS : (c + 1) * ROWS, :] = keys[:, c * 128 : (c + 1) * 128]
        out_ref[k, LAT // 128 * ROWS :, :] = rope


def unpack(keys_ref, part):
    latents, ropes = [], []
    for k in range(HEADS):
        rows = [c * ROWS + part * HALF for c in range(LAT // 128)]
        latents.append(jnp.concatenate([keys_ref[k, r : r + HALF, :] for r in rows], axis=1))
        ropes.append(keys_ref[k, LAT // 128 * ROWS :, part * ROPE : (part + 1) * ROPE])
    return jnp.concatenate(latents, axis=0), jnp.concatenate(ropes, axis=0)


class Rows:
    def __init__(self, where_ref, q_ref, m_ref, l_ref, acc_ref, scale):
        self.chip, self.core = where_ref[1], where_ref[2]
        self.q_ref, self.m_ref, self.l_ref, self.acc_ref = q_ref, m_ref, l_ref, acc_ref
        self.scale = scale

    def chunk(self, keys_ref, part, key_core, fresh):
        latent, rope = unpack(keys_ref, part)
        scores = dot(jnp.concatenate([latent, rope], axis=1), self.q_ref[...]) * self.scale
        if key_core is not None:
            query = lax.broadcasted_iota(jnp.int32, (1, ALL), 1) % ROWS
            key = lax.broadcasted_iota(jnp.int32, (KEYS, 1), 0)
            ahead = (2 * self.chip + self.core) * ROWS + query
            place = (2 * (part * CHIPS // 2 + key % HALF // PIECE) + key_core) * ROWS
            place += key // HALF * PIECE + key % PIECE
            scores = jnp.where(place <= ahead, scores, UNSEEN)
        top = jnp.max(scores, axis=0, keepdims=True)
        new = jnp.broadcast_to(top, (8, ALL)) if fresh else jnp.maximum(self.m_ref[...], top)
        weights = jnp.exp2(scores - new[:1])
        total = jnp.sum(weights.reshape(KEYS // 8, 8, ALL), axis=0)
        attended = dot(latent.T, weights.astype(BF16))
        if not fresh:
            factor = jnp.exp2(self.m_ref[...] - new)
            total += self.l_ref[...] * factor
            attended += self.acc_ref[...] * factor[:1]
        self.m_ref[...] = new
        self.l_ref[...] = total
        self.acc_ref[...] = attended

    def head_out(self, h, absorb_ref):
        columns = slice(h * ROWS, (h + 1) * ROWS)
        total = jnp.sum(self.l_ref[:, columns], axis=0, keepdims=True)
        attended = (self.acc_ref[:, columns] * (1.0 / total)).astype(BF16)
        return dot_first(absorb_ref[h], attended), self.m_ref[:1, columns] + jnp.log2(total)


def first_kernel(scale, where_ref, own_ref, partner_ref, keys_ref, *state):
    far_chip = where_ref[1] >= CHIPS // 2

    @pl.when(where_ref[0] == 0)
    def _():
        rows = Rows(where_ref, partner_ref, *state, scale)
        rows.chunk(keys_ref, 0, None, True)
        rows.chunk(keys_ref, 1, None, False)

    @pl.when(where_ref[0] == 1)
    def _():
        rows = Rows(where_ref, own_ref, *state, scale)
        rows.chunk(keys_ref, 0, where_ref[2], True)

        @pl.when(far_chip)
        def _():
            rows.chunk(keys_ref, 1, where_ref[2], False)


def second_kernel(scale, where_ref, partner_ref, keys_ref, absorb_ref, *refs):
    part_ref, *state = refs[3:]

    @pl.when(where_ref[0] == 0)
    def _():
        rows = Rows(where_ref, partner_ref, *state, scale)
        rows.chunk(keys_ref, 0, None, False)
        rows.chunk(keys_ref, 1, None, False)
        outs = [rows.head_out(h, absorb_ref) for h in range(HEADS)]
        for h, (out, _) in enumerate(outs):
            part_ref[h * VDIM : (h + 1) * VDIM, :] = out.astype(BF16)
        logs = jnp.concatenate([log for _, log in outs], axis=0)
        terms = [t.astype(F32) for t in thirds(logs)] + [jnp.zeros_like(logs)]
        part_ref[HEADS * VDIM :, :] = jnp.concatenate(terms, axis=0).astype(BF16)


def third_kernel(scale, where_ref, own_ref, keys_ref, others_ref, values_ref, pattern_ref, *refs):
    *state, dense_ref = refs[3:]
    lower = where_ref[0] == 0
    core = where_ref[2]
    rows = Rows(where_ref, own_ref, *state, scale)

    def weights(*steps):
        for step in steps:
            columns = slice(step * COLS, (step + 1) * COLS)
            densify(values_ref.at[:, columns], pattern_ref.at[:, columns], dense_ref.at[:, columns])

    @pl.when(where_ref[1] >= CHIPS // 2)
    def _():
        @pl.when(lower)
        def _():
            rows.chunk(keys_ref, 0, core, True)
            rows.chunk(keys_ref, 1, core, False)

        weights(0, 1)
        rows.chunk(others_ref, 0, 1 - core, False)
        weights(2, 3)
        rows.chunk(others_ref, 1, 1 - core, False)

    @pl.when(where_ref[1] < CHIPS // 2)
    def _():
        @pl.when(lower)
        def _():
            rows.chunk(keys_ref, 0, core, True)

        weights(0, 1, 2, 3)
        rows.chunk(others_ref, 0, 1 - core, False)


def output_kernel(
    where_ref, m_ref, l_ref, acc_ref, part_ref, absorb_ref, down_ref, up_ref, dense_ref,
    out_ref,
):
    upper = where_ref[0]
    rows = Rows(where_ref, None, m_ref, l_ref, acc_ref, None)
    logs = part_ref[HEADS * VDIM :, :].astype(F32)
    logs = logs[:HEADS] + logs[HEADS : 2 * HEADS] + logs[2 * HEADS : 3 * HEADS]
    mine = [rows.head_out(h, absorb_ref) for h in range(HEADS)]
    outs = []
    for h, (own, log) in enumerate(mine):
        other_log = jnp.where(upper == 1, logs[h : h + 1], -jnp.inf)
        top = jnp.maximum(log, other_log)
        weight, other_weight = jnp.exp2(log - top), jnp.exp2(other_log - top)
        share = 1.0 / (weight + other_weight)
        other = part_ref[h * VDIM : (h + 1) * VDIM, :].astype(F32)
        outs.append((own * (weight * share) + other * (other_weight * share)).astype(BF16))
    order = by_slot()
    flat = jnp.concatenate([dot_first(out, order).astype(BF16) for out in outs], axis=1)
    lowrank = dot(down_ref[...], jnp.concatenate(outs, axis=0))
    low = jnp.concatenate(thirds(lowrank.T), axis=1)
    for c in range(0, out_ref.shape[0], COLS):
        up = up_ref[:, c : c + COLS]
        terms = dot(flat, dense_ref[:, c : c + COLS])
        terms += dot(low, jnp.concatenate([up] * 3, axis=0))
        out_ref[c : c + COLS, :] = terms.T.astype(BF16)


def sum_kernel(parts_ref, out_ref):
    total = parts_ref[0].astype(F32)
    for h in range(1, HEADS):
        total += parts_ref[h].astype(F32)
    out_ref[...] = total


def shape(*dims, dtype=F32):
    return jax.ShapeDtypeStruct(dims, dtype)


def params(mib):
    return pltpu.CompilerParams(vmem_limit_bytes=mib * MIB)


def cost(flops, nbytes, exps=0):
    return pl.CostEstimate(flops=flops, bytes_accessed=nbytes, transcendentals=exps)


VMEM = pl.BlockSpec(memory_space=pltpu.VMEM)
SMEM = pl.BlockSpec(memory_space=pltpu.SMEM)
ANY = pl.BlockSpec(memory_space=pl.ANY)


def tables(positions):
    half = ROPE // 2
    freqs = 10000.0 ** (-jnp.arange(half, dtype=F32) / half)
    angles = positions.astype(F32)[:, None] * freqs
    cos, sin = jnp.cos(angles), jnp.sin(angles)
    return jnp.concatenate([cos, cos, -sin, sin], axis=1)


def local(
    tokens, kv_values, kv_pattern, kv_down, kv_up, kv_gain, queries, absorb_k, absorb_v,
    o_values, o_pattern, o_down, o_up,
):
    ctx = lax.axis_index("ctx")
    head = lax.axis_index("head")
    upper = ctx // (2 * CHIPS)
    where = jnp.stack([upper, (ctx // 2) % CHIPS, ctx % 2, head]).astype(jnp.int32)
    scale = LOG2E / math.sqrt(queries.shape[2])
    out_cols = o_values.shape[1]
    rank = o_down.shape[1]

    columns = jnp.transpose(queries, (1, 2, 0))
    partner = lax.ppermute(columns, "ctx", [(i + 2 * CHIPS, i) for i in range(2 * CHIPS)])

    raw = pl.pallas_call(
        project_kernel,
        out_shape=shape(HEADS, PIECE * WIDTH // 128, 128),
        in_specs=[ANY] * 5,
        out_specs=VMEM,
        scratch_shapes=[
            pltpu.VMEM(tokens.shape, BF16),
            pltpu.VMEM(kv_values.shape, BF16),
            pltpu.VMEM(kv_pattern.shape, jnp.int32),
            pltpu.VMEM(kv_down.shape[::-1], BF16),
            pltpu.VMEM(kv_up.shape, BF16),
            pltpu.VMEM((tokens.shape[1], WIDTH), BF16),
            pltpu.SemaphoreType.DMA((5,)),
        ],
        compiler_params=params(56),
        name="project",
    )(tokens, kv_values, kv_pattern, kv_down.T, kv_up)
    parts = lax.all_to_all(raw, "head", 0, 0, tiled=True)

    positions = ctx * ROWS + jnp.arange(ROWS, dtype=jnp.int32)
    table = tables(positions)
    partner_table = tables(positions + 2 * CHIPS * ROWS)

    def query(x, t):
        return pl.pallas_call(
            query_kernel,
            out_shape=(shape(WIDTH, ALL, dtype=BF16), shape(8, 128)),
            in_specs=[VMEM] * 3,
            out_specs=(VMEM, VMEM),
            compiler_params=params(16),
            cost_estimate=cost(2 * ALL * NOPE * LAT, 4 * MIB),
            name="query",
        )(x, absorb_k, t.T)

    own_query, own_token = query(columns, table)
    partner_query, partner_token = query(partner, partner_table)

    piece = pl.pallas_call(
        finish_kernel,
        out_shape=shape(CHIPS, PIECE, WIDE, dtype=BF16),
        in_specs=[SMEM] + [VMEM] * 4,
        out_specs=VMEM,
        compiler_params=params(16),
        name="finish",
    )(where, parts, kv_gain.reshape(1, LAT), table, own_token)

    along_z = [
        [(u * CHIPS + chip) * 2 + core for chip in range(CHIPS)]
        for u in range(2)
        for core in range(2)
    ]
    column = lax.all_to_all(piece, "ctx", 0, 0, tiled=True, axis_index_groups=along_z)
    packed = pl.pallas_call(
        pack_kernel,
        out_shape=shape(HEADS, PACKED, 128, dtype=BF16),
        in_specs=[VMEM] * 2,
        out_specs=VMEM,
        compiler_params=params(16),
        name="pack",
    )(column, partner_token)
    keys = lax.all_to_all(packed, "head", 0, 0, tiled=True)
    others = lax.ppermute(keys, "ctx", [(i, i ^ 1) for i in range(CTX)])

    state = (shape(8, ALL), shape(8, ALL), shape(LAT, ALL))
    scores = ALL * CHIPS * ROWS
    work = cost(2 * scores * (WIDTH + LAT), 8 * MIB, scores)
    first = pl.pallas_call(
        functools.partial(first_kernel, scale),
        out_shape=state,
        in_specs=[SMEM, VMEM, VMEM, VMEM],
        out_specs=(VMEM,) * 3,
        compiler_params=params(32),
        cost_estimate=work,
        name="first",
    )(where, own_query, partner_query, keys)
    part, *second = pl.pallas_call(
        functools.partial(second_kernel, scale),
        out_shape=(shape(HEADS * VDIM + 4 * HEADS, ROWS, dtype=BF16),) + state,
        in_specs=[SMEM] + [VMEM] * 6,
        out_specs=(VMEM,) * 4,
        input_output_aliases={4: 1, 5: 2, 6: 3},
        compiler_params=params(32),
        cost_estimate=work,
        name="second",
    )(where, partner_query, others, absorb_v, *first)
    received = lax.ppermute(part, "ctx", [(i, i + 2 * CHIPS) for i in range(2 * CHIPS)])
    *own, dense = pl.pallas_call(
        functools.partial(third_kernel, scale),
        out_shape=state + (shape(2 * o_values.shape[0], out_cols, dtype=BF16),),
        in_specs=[SMEM] + [VMEM] * 8,
        out_specs=(VMEM,) * 4,
        input_output_aliases={6: 0, 7: 1, 8: 2},
        compiler_params=params(32),
        cost_estimate=work,
        name="third",
    )(where, own_query, keys, others, o_values, o_pattern, *second)

    terms = pl.pallas_call(
        output_kernel,
        out_shape=shape(out_cols, ROWS, dtype=BF16),
        in_specs=[SMEM] + [VMEM] * 8,
        out_specs=VMEM,
        compiler_params=params(32),
        cost_estimate=cost(2 * ROWS * HEADS * VDIM * out_cols, 8 * MIB),
        name="output",
    )(where, *own, received, absorb_v, o_down.T, o_up, dense)
    shares = lax.all_to_all(
        terms.reshape(HEADS, out_cols // HEADS, ROWS), "head", 0, 0, tiled=True
    )
    return pl.pallas_call(
        sum_kernel,
        out_shape=shape(out_cols // HEADS, ROWS),
        in_specs=[VMEM],
        out_specs=VMEM,
        compiler_params=params(16),
        name="total",
    )(shares).T


def solution(mesh):
    in_specs = (
        P("ctx", "head"),
        P("head", None),
        P("head", None),
        P("head", None),
        P(),
        P(),
        P("ctx", "head", None),
        P("head", None, None),
        P("head", None, None),
        P("head", None),
        P("head", None),
        P("head", None),
        P(),
    )
    out_specs = P("ctx", "head")
    return jax.shard_map(local, mesh=mesh, in_specs=in_specs, out_specs=out_specs, check_vma=False)
```

```python
import functools
import math

import jax
import jax.numpy as jnp
from jax import lax
from jax.experimental import pallas as pl
from jax.experimental.pallas import tpu as pltpu
from jax.sharding import PartitionSpec as P

BF16 = jnp.bfloat16
F32 = jnp.float32
MIB = 1024 * 1024
HEADS = 8
ROWS = 128
ALL = HEADS * ROWS
PIECE = ROWS // HEADS
LAT = 512
ROPE = 64
WIDTH = LAT + ROPE
NOPE = 128
VDIM = 128
CTX = 32
CHIPS = 8
PACKED = ROWS * WIDTH // 128
HALF = ROWS // 2
KEYS = HEADS * HALF
WIDE = 640
UNSEEN = -1e30
COLS = 640
LOG2E = 1.4426950408889634


def dot(a, b):
    return jnp.dot(a, b, preferred_element_type=F32)


def dot_first(a, b):
    return lax.dot_general(a, b, (((0,), (0,)), ((), ())), preferred_element_type=F32)


def dot_last(a, b):
    return lax.dot_general(a, b, (((1,), (1,)), ((), ())), preferred_element_type=F32)


def unpair(count):
    half = count // 2
    rows = lax.broadcasted_iota(jnp.int32, (count, count), 0)
    columns = lax.broadcasted_iota(jnp.int32, (count, count), 1)
    wanted = jnp.where(rows < half, 2 * rows, 2 * (rows - half) + 1)
    return jnp.where(columns == wanted, 1.0, 0.0).astype(BF16)


def by_slot():
    rows = lax.broadcasted_iota(jnp.int32, (128, 128), 0)
    columns = lax.broadcasted_iota(jnp.int32, (128, 128), 1)
    return jnp.where(rows == 4 * (columns % 32) + columns // 32, 1.0, 0.0).astype(BF16)


def densify(values_ref, pattern_ref, dense_ref):
    total = values_ref.shape[0]
    zero = jnp.zeros((), BF16)
    begin = 0
    while begin < total:
        count = min(256, total - begin)
        half = count // 2
        pair = dot(unpair(count), values_ref[begin : begin + count, :]).astype(BF16)
        v0, v1 = pair[:half], pair[half:]
        p = pattern_ref[begin // 2 : begin // 2 + half, :].astype(BF16)
        is_0, is_1, is_3, is_5 = (p == jnp.asarray(k, BF16) for k in (0, 1, 3, 5))
        from_0 = p < jnp.asarray(3, BF16)
        later = jnp.where(from_0, zero, v0)
        to_2 = is_1 | is_3
        slots = (
            jnp.where(from_0, v0, zero),
            jnp.where(is_0, v1, jnp.where(is_5, zero, later)),
            jnp.where(to_2, v1, jnp.where(is_5, later, zero)),
            jnp.where(is_0 | to_2, zero, v1),
        )
        for k, slot in enumerate(slots):
            for b in range(half // 32):
                row = 2 * begin + 128 * b + 32 * k
                dense_ref[row : row + 32, :] = slot[32 * b : 32 * b + 32]
        begin += count


def position():
    ctx = lax.axis_index("ctx")
    return ctx >> 4, (ctx >> 1) & 7, ctx & 1, lax.axis_index("head")


def thirds(x):
    high = x.astype(BF16)
    rest = x - high.astype(F32)
    middle = rest.astype(BF16)
    low = (rest - middle.astype(F32)).astype(BF16)
    return high, middle, low


def project_kernel(
    tokens_hbm, values_hbm, pattern_hbm, down_hbm, up_hbm,
    raw_ref, tokens_ref, values_ref, pattern_ref, down_ref, up_ref, dense_ref, sems,
):
    copies = [
        pltpu.make_async_copy(source, target, sems.at[n])
        for n, (source, target) in enumerate(
            (
                (tokens_hbm, tokens_ref),
                (down_hbm, down_ref),
                (up_hbm, up_ref),
                (values_hbm, values_ref),
                (pattern_hbm, pattern_ref),
            )
        )
    ]
    for copy in copies:
        copy.start()
    for copy in copies[:3]:
        copy.wait()
    order = by_slot()
    tokens = tokens_ref[...]
    parts = [dot(tokens[:, b : b + 128], order).astype(BF16) for b in range(0, tokens.shape[1], 128)]
    low = jnp.concatenate(thirds(dot_last(tokens, down_ref[...])), axis=1)
    raw = dot(low, jnp.concatenate([up_ref[...]] * 3, axis=0))
    for copy in copies[3:]:
        copy.wait()
    densify(values_ref, pattern_ref, dense_ref)
    raw += dot(jnp.concatenate(parts, axis=1), dense_ref[...])
    for h in range(HEADS):
        piece = raw[h * PIECE : (h + 1) * PIECE]
        for c in range(LAT // 128):
            raw_ref[h, c * PIECE : (c + 1) * PIECE, :] = piece[:, c * 128 : (c + 1) * 128]
        rope = piece[:, LAT:]
        raw_ref[h, LAT // 128 * PIECE :, :] = jnp.concatenate(
            [rope[: PIECE // 2], rope[PIECE // 2 :]], axis=1
        )


def query_kernel(queries_ref, absorb_ref, table_ref, out_ref, token_ref):
    token_ref[...] = jnp.zeros(token_ref.shape, F32)
    half = ROPE // 2
    cos, sin = table_ref[:ROPE, :], table_ref[ROPE:, :]
    for h in range(HEADS):
        columns = slice(h * ROWS, (h + 1) * ROWS)
        out_ref[:LAT, columns] = dot_first(absorb_ref[h], queries_ref[h, :NOPE, :]).astype(BF16)
        x = queries_ref[h, NOPE:, :].astype(F32)
        swapped = jnp.concatenate([x[half:], x[:half]], axis=0)
        out_ref[LAT:, columns] = (x * cos + swapped * sin).astype(BF16)


def finish_kernel(parts_ref, gain_ref, table_ref, *refs):
    out_ref = refs[-1]
    raw = parts_ref[0]
    for h in range(1, HEADS):
        raw += parts_ref[h]
    latent = jnp.concatenate(
        [raw[c * PIECE : (c + 1) * PIECE] for c in range(LAT // 128)], axis=1
    )
    rope = raw[LAT // 128 * PIECE :]
    meansq = jnp.mean(latent * latent, axis=-1, keepdims=True)
    normed = (latent * lax.rsqrt(meansq + 1e-06) * gain_ref[...]).astype(BF16)
    table = table_ref[pl.ds(pl.multiple_of(position()[3] * PIECE, PIECE), PIECE), :]
    x = jnp.concatenate([rope[:, :ROPE], rope[:, ROPE:]], axis=0)
    half = ROPE // 2
    swapped = jnp.concatenate([x[:, half:], x[:, :half]], axis=1)
    turned = (x * table[:, :ROPE] + swapped * table[:, ROPE:]).astype(BF16)
    for c in range(CHIPS):
        out_ref[c, :, :LAT] = normed
        out_ref[c, :, LAT:WIDTH] = turned
        out_ref[c, :, WIDTH:] = jnp.zeros((PIECE, WIDE - WIDTH), BF16)


def pack_kernel(column_ref, *refs):
    out_ref = refs[-1]
    keys = column_ref[...].reshape(ROWS, WIDE)
    rope = keys[:, LAT:WIDTH]
    rope = jnp.concatenate([rope[: ROWS // 2], rope[ROWS // 2 :]], axis=1)
    for k in range(HEADS):
        for c in range(LAT // 128):
            out_ref[k, c * ROWS : (c + 1) * ROWS, :] = keys[:, c * 128 : (c + 1) * 128]
        out_ref[k, LAT // 128 * ROWS :, :] = rope


def unpack(keys_ref, part):
    latents, ropes = [], []
    for k in range(HEADS):
        rows = [c * ROWS + part * HALF for c in range(LAT // 128)]
        latents.append(jnp.concatenate([keys_ref[k, r : r + HALF, :] for r in rows], axis=1))
        ropes.append(keys_ref[k, LAT // 128 * ROWS :, part * ROPE : (part + 1) * ROPE])
    return jnp.concatenate(latents, axis=0), jnp.concatenate(ropes, axis=0)


class Rows:
    def __init__(self, q_ref, m_ref, l_ref, acc_ref, scale):
        _, self.chip, self.core, _ = position()
        self.q_ref, self.m_ref, self.l_ref, self.acc_ref = q_ref, m_ref, l_ref, acc_ref
        self.scale = scale

    def chunk(self, keys_ref, part, key_core, fresh):
        latent, rope = unpack(keys_ref, part)
        scores = dot(jnp.concatenate([latent, rope], axis=1), self.q_ref[...]) * self.scale
        if key_core is not None:
            query = lax.broadcasted_iota(jnp.int32, (1, ALL), 1) % ROWS
            key = lax.broadcasted_iota(jnp.int32, (KEYS, 1), 0)
            ahead = (2 * self.chip + self.core) * ROWS + query
            place = (2 * (part * CHIPS // 2 + key % HALF // PIECE) + key_core) * ROWS
            place += key // HALF * PIECE + key % PIECE
            scores = jnp.where(place <= ahead, scores, UNSEEN)
        top = jnp.max(scores, axis=0, keepdims=True)
        new = jnp.broadcast_to(top, (8, ALL)) if fresh else jnp.maximum(self.m_ref[...], top)
        weights = jnp.exp2(scores - new[:1])
        total = jnp.sum(weights.reshape(KEYS // 8, 8, ALL), axis=0)
        attended = dot(latent.T, weights.astype(BF16))
        if not fresh:
            factor = jnp.exp2(self.m_ref[...] - new)
            total += self.l_ref[...] * factor
            attended += self.acc_ref[...] * factor[:1]
        self.m_ref[...] = new
        self.l_ref[...] = total
        self.acc_ref[...] = attended

    def head_out(self, h, absorb_ref):
        columns = slice(h * ROWS, (h + 1) * ROWS)
        total = jnp.sum(self.l_ref[:, columns], axis=0, keepdims=True)
        attended = (self.acc_ref[:, columns] * (1.0 / total)).astype(BF16)
        return dot_first(absorb_ref[h], attended), self.m_ref[:1, columns] + jnp.log2(total)


def first_kernel(scale, own_ref, partner_ref, keys_ref, *state):
    half, chip, core, _ = position()

    @pl.when(half == 0)
    def _():
        rows = Rows(partner_ref, *state, scale)
        rows.chunk(keys_ref, 0, None, True)
        rows.chunk(keys_ref, 1, None, False)

    @pl.when(half == 1)
    def _():
        rows = Rows(own_ref, *state, scale)
        rows.chunk(keys_ref, 0, core, True)

        @pl.when(chip >= CHIPS // 2)
        def _():
            rows.chunk(keys_ref, 1, core, False)


def second_kernel(scale, partner_ref, keys_ref, absorb_ref, *refs):
    part_ref, *state = refs[3:]
    half = position()[0]

    @pl.when(half == 0)
    def _():
        rows = Rows(partner_ref, *state, scale)
        rows.chunk(keys_ref, 0, None, False)
        rows.chunk(keys_ref, 1, None, False)
        outs = [rows.head_out(h, absorb_ref) for h in range(HEADS)]
        for h, (out, _) in enumerate(outs):
            part_ref[h * VDIM : (h + 1) * VDIM, :] = out.astype(BF16)
        logs = jnp.concatenate([log for _, log in outs], axis=0)
        terms = [t.astype(F32) for t in thirds(logs)] + [jnp.zeros_like(logs)]
        part_ref[HEADS * VDIM :, :] = jnp.concatenate(terms, axis=0).astype(BF16)


def third_kernel(
    scale, own_ref, keys_ref, others_ref, values_ref, pattern_ref, absorb_ref, *refs
):
    out_ref, log_ref, dense_ref, *state = refs[3:]
    half, chip, core, _ = position()
    lower = half == 0
    rows = Rows(own_ref, *state, scale)

    def weights(*steps):
        for step in steps:
            columns = slice(step * COLS, (step + 1) * COLS)
            densify(values_ref.at[:, columns], pattern_ref.at[:, columns], dense_ref.at[:, columns])

    @pl.when(chip >= CHIPS // 2)
    def _():
        @pl.when(lower)
        def _():
            rows.chunk(keys_ref, 0, None, True)
            rows.chunk(keys_ref, 1, core, False)

        weights(0, 1)
        rows.chunk(others_ref, 0, None, False)
        weights(2, 3)
        rows.chunk(others_ref, 1, 1 - core, False)

    @pl.when(chip < CHIPS // 2)
    def _():
        @pl.when(lower)
        def _():
            rows.chunk(keys_ref, 0, core, True)

        weights(0, 1, 2, 3)
        rows.chunk(others_ref, 0, 1 - core, False)

    outs = [rows.head_out(h, absorb_ref) for h in range(HEADS)]
    for h, (out, _) in enumerate(outs):
        out_ref[h * VDIM : (h + 1) * VDIM, :] = out
    log_ref[...] = jnp.concatenate([log for _, log in outs], axis=0)


def output_kernel(mine_ref, log_ref, part_ref, down_ref, up_ref, dense_ref, out_ref):
    upper = position()[0]
    logs = part_ref[HEADS * VDIM :, :].astype(F32)
    logs = logs[:HEADS] + logs[HEADS : 2 * HEADS] + logs[2 * HEADS : 3 * HEADS]
    logs = jnp.where(upper == 1, logs, -jnp.inf)
    own_logs = log_ref[...]
    top = jnp.maximum(own_logs, logs)
    own_weights, weights = jnp.exp2(own_logs - top), jnp.exp2(logs - top)
    share = 1.0 / (own_weights + weights)
    own_weights, weights = own_weights * share, weights * share
    outs = []
    for h in range(HEADS):
        span = slice(h * VDIM, (h + 1) * VDIM)
        other = part_ref[span, :].astype(F32) * weights[h : h + 1]
        outs.append((mine_ref[span, :] * own_weights[h : h + 1] + other).astype(BF16))
    order = by_slot()
    flat = jnp.concatenate([dot_first(out, order).astype(BF16) for out in outs], axis=1)
    lowrank = dot(down_ref[...], jnp.concatenate(outs, axis=0))
    low = jnp.concatenate(thirds(lowrank.T), axis=1)
    for c in range(0, out_ref.shape[0], COLS):
        up = up_ref[:, c : c + COLS]
        terms = dot(flat, dense_ref[:, c : c + COLS])
        terms += dot(low, jnp.concatenate([up] * 3, axis=0))
        out_ref[c : c + COLS, :] = terms.T.astype(BF16)


def sum_kernel(parts_ref, out_ref):
    total = parts_ref[0].astype(F32)
    for h in range(1, HEADS):
        total += parts_ref[h].astype(F32)
    out_ref[...] = total


def shape(*dims, dtype=F32):
    return jax.ShapeDtypeStruct(dims, dtype)


def params(mib):
    return pltpu.CompilerParams(vmem_limit_bytes=mib * MIB)


def cost(flops, nbytes, exps=0):
    return pl.CostEstimate(flops=flops, bytes_accessed=nbytes, transcendentals=exps)


VMEM = pl.BlockSpec(memory_space=pltpu.VMEM)
ANY = pl.BlockSpec(memory_space=pl.ANY)


def tables(positions):
    half = ROPE // 2
    freqs = 10000.0 ** (-jnp.arange(half, dtype=F32) / half)
    angles = positions.astype(F32)[:, None] * freqs
    cos, sin = jnp.cos(angles), jnp.sin(angles)
    return jnp.concatenate([cos, cos, -sin, sin], axis=1)


def local(
    tokens, kv_values, kv_pattern, kv_down, kv_up, kv_gain, queries, absorb_k, absorb_v,
    o_values, o_pattern, o_down, o_up,
):
    ctx = lax.axis_index("ctx")
    scale = LOG2E / math.sqrt(queries.shape[2])
    out_cols = o_values.shape[1]
    rank = o_down.shape[1]

    columns = jnp.transpose(queries, (1, 2, 0))
    partner = lax.ppermute(columns, "ctx", [(i + 2 * CHIPS, i) for i in range(2 * CHIPS)])

    raw = pl.pallas_call(
        project_kernel,
        out_shape=shape(HEADS, PIECE * WIDTH // 128, 128),
        in_specs=[ANY] * 5,
        out_specs=VMEM,
        scratch_shapes=[
            pltpu.VMEM(tokens.shape, BF16),
            pltpu.VMEM(kv_values.shape, BF16),
            pltpu.VMEM(kv_pattern.shape, jnp.int32),
            pltpu.VMEM(kv_down.shape[::-1], BF16),
            pltpu.VMEM(kv_up.shape, BF16),
            pltpu.VMEM((tokens.shape[1], WIDTH), BF16),
            pltpu.SemaphoreType.DMA((5,)),
        ],
        compiler_params=params(56),
        name="project",
    )(tokens, kv_values, kv_pattern, kv_down.T, kv_up)
    parts = lax.all_to_all(raw, "head", 0, 0, tiled=True)

    positions = ctx * ROWS + jnp.arange(ROWS, dtype=jnp.int32)
    table = tables(positions)
    partner_table = tables(positions + 2 * CHIPS * ROWS)

    def query(x, t):
        return pl.pallas_call(
            query_kernel,
            out_shape=(shape(WIDTH, ALL, dtype=BF16), shape(8, 128)),
            in_specs=[VMEM] * 3,
            out_specs=(VMEM, VMEM),
            compiler_params=params(16),
            cost_estimate=cost(2 * ALL * NOPE * LAT, 4 * MIB),
            name="query",
        )(x, absorb_k, t.T)

    own_query, own_token = query(columns, table)
    partner_query, partner_token = query(partner, partner_table)

    piece = pl.pallas_call(
        finish_kernel,
        out_shape=shape(CHIPS, PIECE, WIDE, dtype=BF16),
        in_specs=[VMEM] * 4,
        out_specs=VMEM,
        compiler_params=params(16),
        name="finish",
    )(parts, kv_gain.reshape(1, LAT), table, own_token)

    along_z = [
        [(u * CHIPS + chip) * 2 + core for chip in range(CHIPS)]
        for u in range(2)
        for core in range(2)
    ]
    column = lax.all_to_all(piece, "ctx", 0, 0, tiled=True, axis_index_groups=along_z)
    packed = pl.pallas_call(
        pack_kernel,
        out_shape=shape(HEADS, PACKED, 128, dtype=BF16),
        in_specs=[VMEM] * 2,
        out_specs=VMEM,
        compiler_params=params(16),
        name="pack",
    )(column, partner_token)
    keys = lax.all_to_all(packed, "head", 0, 0, tiled=True)
    others = lax.ppermute(keys, "ctx", [(i, i ^ 1) for i in range(CTX)])

    state = (shape(8, ALL), shape(8, ALL), shape(LAT, ALL))
    scores = ALL * CHIPS * ROWS
    work = cost(2 * scores * (WIDTH + LAT), 8 * MIB, scores)
    first = pl.pallas_call(
        functools.partial(first_kernel, scale),
        out_shape=state,
        in_specs=[VMEM] * 3,
        out_specs=(VMEM,) * 3,
        compiler_params=params(32),
        cost_estimate=work,
        name="first",
    )(own_query, partner_query, keys)
    part, *second = pl.pallas_call(
        functools.partial(second_kernel, scale),
        out_shape=(shape(HEADS * VDIM + 4 * HEADS, ROWS, dtype=BF16),) + state,
        in_specs=[VMEM] * 6,
        out_specs=(VMEM,) * 4,
        input_output_aliases={3: 1, 4: 2, 5: 3},
        compiler_params=params(32),
        cost_estimate=work,
        name="second",
    )(partner_query, others, absorb_v, *first)
    received = lax.ppermute(part, "ctx", [(i, i + 2 * CHIPS) for i in range(2 * CHIPS)])
    mine, logs, dense, *_ = pl.pallas_call(
        functools.partial(third_kernel, scale),
        out_shape=(
            shape(HEADS * VDIM, ROWS),
            shape(HEADS, ROWS),
            shape(2 * o_values.shape[0], out_cols, dtype=BF16),
        )
        + state,
        in_specs=[VMEM] * 9,
        out_specs=(VMEM,) * 6,
        input_output_aliases={6: 3, 7: 4, 8: 5},
        compiler_params=params(32),
        cost_estimate=work,
        name="third",
    )(own_query, keys, others, o_values, o_pattern, absorb_v, *second)

    terms = pl.pallas_call(
        output_kernel,
        out_shape=shape(out_cols, ROWS, dtype=BF16),
        in_specs=[VMEM] * 6,
        out_specs=VMEM,
        compiler_params=params(32),
        cost_estimate=cost(2 * ROWS * HEADS * VDIM * out_cols, 8 * MIB),
        name="output",
    )(mine, logs, received, o_down.T, o_up, dense)
    shares = lax.all_to_all(
        terms.reshape(HEADS, out_cols // HEADS, ROWS), "head", 0, 0, tiled=True
    )
    return pl.pallas_call(
        sum_kernel,
        out_shape=shape(out_cols // HEADS, ROWS),
        in_specs=[VMEM],
        out_specs=VMEM,
        compiler_params=params(16),
        name="total",
    )(shares).T


def solution(mesh):
    in_specs = (
        P("ctx", "head"),
        P("head", None),
        P("head", None),
        P("head", None),
        P(),
        P(),
        P("ctx", "head", None),
        P("head", None, None),
        P("head", None, None),
        P("head", None),
        P("head", None),
        P("head", None),
        P(),
    )
    out_specs = P("ctx", "head")
    return jax.shard_map(local, mesh=mesh, in_specs=in_specs, out_specs=out_specs, check_vma=False)
```

```python
import functools
import math

import jax
import jax.numpy as jnp
from jax import lax
from jax.experimental import pallas as pl
from jax.experimental.pallas import tpu as pltpu
from jax.sharding import PartitionSpec as P

BF16 = jnp.bfloat16
F32 = jnp.float32
MIB = 1024 * 1024
HEADS = 8
ROWS = 128
ALL = HEADS * ROWS
PIECE = ROWS // HEADS
LAT = 512
ROPE = 64
WIDTH = LAT + ROPE
NOPE = 128
VDIM = 128
CTX = 32
CHIPS = 8
ORDER = (4, 5, 6, 7, 0, 1, 2, 3)
FIRST = 4
PLACES = tuple((place + FIRST) % HEADS for place in range(HEADS))
PACKED = ROWS * WIDTH // 128
HALF = ROWS // 2
KEYS = HEADS * HALF
WIDE = 640
UNSEEN = -1e30
COLS = 640
LOG2E = 1.4426950408889634


def dot(a, b):
    return jnp.dot(a, b, preferred_element_type=F32)


def dot_first(a, b):
    return lax.dot_general(a, b, (((0,), (0,)), ((), ())), preferred_element_type=F32)


def dot_last(a, b):
    return lax.dot_general(a, b, (((1,), (1,)), ((), ())), preferred_element_type=F32)


def unpair(count):
    half = count // 2
    rows = lax.broadcasted_iota(jnp.int32, (count, count), 0)
    columns = lax.broadcasted_iota(jnp.int32, (count, count), 1)
    wanted = jnp.where(rows < half, 2 * rows, 2 * (rows - half) + 1)
    return jnp.where(columns == wanted, 1.0, 0.0).astype(BF16)


def by_slot():
    rows = lax.broadcasted_iota(jnp.int32, (128, 128), 0)
    columns = lax.broadcasted_iota(jnp.int32, (128, 128), 1)
    return jnp.where(rows == 4 * (columns % 32) + columns // 32, 1.0, 0.0).astype(BF16)


def densify(values_ref, pattern_ref, dense_ref):
    total = values_ref.shape[0]
    zero = jnp.zeros((), BF16)
    begin = 0
    while begin < total:
        count = min(256, total - begin)
        half = count // 2
        pair = dot(unpair(count), values_ref[begin : begin + count, :]).astype(BF16)
        v0, v1 = pair[:half], pair[half:]
        p = pattern_ref[begin // 2 : begin // 2 + half, :].astype(BF16)
        is_0, is_1, is_3, is_5 = (p == jnp.asarray(k, BF16) for k in (0, 1, 3, 5))
        from_0 = p < jnp.asarray(3, BF16)
        later = jnp.where(from_0, zero, v0)
        to_2 = is_1 | is_3
        slots = (
            jnp.where(from_0, v0, zero),
            jnp.where(is_0, v1, jnp.where(is_5, zero, later)),
            jnp.where(to_2, v1, jnp.where(is_5, later, zero)),
            jnp.where(is_0 | to_2, zero, v1),
        )
        for k, slot in enumerate(slots):
            for b in range(half // 32):
                row = 2 * begin + 128 * b + 32 * k
                dense_ref[row : row + 32, :] = slot[32 * b : 32 * b + 32]
        begin += count


def position():
    ctx = lax.axis_index("ctx")
    return ctx >> 4, (ctx >> 1) & 7, ctx & 1, lax.axis_index("head")


def thirds(x):
    high = x.astype(BF16)
    rest = x - high.astype(F32)
    middle = rest.astype(BF16)
    low = (rest - middle.astype(F32)).astype(BF16)
    return high, middle, low


def project_kernel(
    tokens_hbm, values_hbm, pattern_hbm, down_hbm, up_hbm,
    raw_ref, tokens_ref, values_ref, pattern_ref, down_ref, up_ref, dense_ref, sems,
):
    copies = [
        pltpu.make_async_copy(source, target, sems.at[n])
        for n, (source, target) in enumerate(
            (
                (tokens_hbm, tokens_ref),
                (down_hbm, down_ref),
                (up_hbm, up_ref),
                (values_hbm, values_ref),
                (pattern_hbm, pattern_ref),
            )
        )
    ]
    for copy in copies:
        copy.start()
    for copy in copies[:3]:
        copy.wait()
    order = by_slot()
    tokens = tokens_ref[...]
    parts = [dot(tokens[:, b : b + 128], order).astype(BF16) for b in range(0, tokens.shape[1], 128)]
    low = jnp.concatenate(thirds(dot_last(tokens, down_ref[...])), axis=1)
    raw = dot(low, jnp.concatenate([up_ref[...]] * 3, axis=0))
    for copy in copies[3:]:
        copy.wait()
    densify(values_ref, pattern_ref, dense_ref)
    raw += dot(jnp.concatenate(parts, axis=1), dense_ref[...])
    for h in range(HEADS):
        piece = raw[PLACES[h] * PIECE : (PLACES[h] + 1) * PIECE]
        for c in range(LAT // 128):
            raw_ref[h, c * PIECE : (c + 1) * PIECE, :] = piece[:, c * 128 : (c + 1) * 128]
        rope = piece[:, LAT:]
        raw_ref[h, LAT // 128 * PIECE :, :] = jnp.concatenate(
            [rope[: PIECE // 2], rope[PIECE // 2 :]], axis=1
        )


def query_kernel(queries_ref, absorb_ref, table_ref, out_ref, token_ref):
    token_ref[...] = jnp.zeros(token_ref.shape, F32)
    half = ROPE // 2
    cos, sin = table_ref[:ROPE, :], table_ref[ROPE:, :]
    for h in range(HEADS):
        columns = slice(h * ROWS, (h + 1) * ROWS)
        out_ref[:LAT, columns] = dot_first(absorb_ref[h], queries_ref[h, :NOPE, :]).astype(BF16)
        x = queries_ref[h, NOPE:, :].astype(F32)
        swapped = jnp.concatenate([x[half:], x[:half]], axis=0)
        out_ref[LAT:, columns] = (x * cos + swapped * sin).astype(BF16)


def finish_kernel(parts_ref, gain_ref, table_ref, *refs):
    out_ref = refs[-1]
    raw = parts_ref[0]
    for h in range(1, HEADS):
        raw += parts_ref[h]
    latent = jnp.concatenate(
        [raw[c * PIECE : (c + 1) * PIECE] for c in range(LAT // 128)], axis=1
    )
    rope = raw[LAT // 128 * PIECE :]
    meansq = jnp.mean(latent * latent, axis=-1, keepdims=True)
    normed = (latent * lax.rsqrt(meansq + 1e-06) * gain_ref[...]).astype(BF16)
    table = table_ref[pl.ds(pl.multiple_of(position()[3] * PIECE, PIECE), PIECE), :]
    x = jnp.concatenate([rope[:, :ROPE], rope[:, ROPE:]], axis=0)
    half = ROPE // 2
    swapped = jnp.concatenate([x[:, half:], x[:, :half]], axis=1)
    turned = (x * table[:, :ROPE] + swapped * table[:, ROPE:]).astype(BF16)
    for c in range(CHIPS):
        out_ref[c, :, :LAT] = normed
        out_ref[c, :, LAT:WIDTH] = turned
        out_ref[c, :, WIDTH:] = jnp.zeros((PIECE, WIDE - WIDTH), BF16)


def pack_kernel(column_ref, *refs):
    out_ref = refs[-1]
    keys = jnp.concatenate([column_ref[ORDER.index(chip)] for chip in range(CHIPS)], axis=0)
    rope = keys[:, LAT:WIDTH]
    rope = jnp.concatenate([rope[: ROWS // 2], rope[ROWS // 2 :]], axis=1)
    for k in range(HEADS):
        for c in range(LAT // 128):
            out_ref[k, c * ROWS : (c + 1) * ROWS, :] = keys[:, c * 128 : (c + 1) * 128]
        out_ref[k, LAT // 128 * ROWS :, :] = rope


def unpack(keys_ref, part):
    latents, ropes = [], []
    for k in range(HEADS):
        rows = [c * ROWS + part * HALF for c in range(LAT // 128)]
        latents.append(jnp.concatenate([keys_ref[k, r : r + HALF, :] for r in rows], axis=1))
        ropes.append(keys_ref[k, LAT // 128 * ROWS :, part * ROPE : (part + 1) * ROPE])
    return jnp.concatenate(latents, axis=0), jnp.concatenate(ropes, axis=0)


class Rows:
    def __init__(self, q_ref, m_ref, l_ref, acc_ref, scale):
        _, self.chip, self.core, _ = position()
        self.q_ref, self.m_ref, self.l_ref, self.acc_ref = q_ref, m_ref, l_ref, acc_ref
        self.scale = scale

    def chunk(self, keys_ref, part, key_core, fresh):
        latent, rope = unpack(keys_ref, part)
        scores = dot(jnp.concatenate([latent, rope], axis=1), self.q_ref[...]) * self.scale
        if key_core is not None:
            query = lax.broadcasted_iota(jnp.int32, (1, ALL), 1) % ROWS
            key = lax.broadcasted_iota(jnp.int32, (KEYS, 1), 0)
            ahead = (2 * self.chip + self.core) * ROWS + query
            place = (2 * (part * CHIPS // 2 + key % HALF // PIECE) + key_core) * ROWS
            place += (key // HALF + FIRST) % HEADS * PIECE + key % PIECE
            scores = jnp.where(place <= ahead, scores, UNSEEN)
        top = jnp.max(scores, axis=0, keepdims=True)
        new = jnp.broadcast_to(top, (8, ALL)) if fresh else jnp.maximum(self.m_ref[...], top)
        weights = jnp.exp2(scores - new[:1])
        total = jnp.sum(weights.reshape(KEYS // 8, 8, ALL), axis=0)
        attended = dot(latent.T, weights.astype(BF16))
        if not fresh:
            factor = jnp.exp2(self.m_ref[...] - new)
            total += self.l_ref[...] * factor
            attended += self.acc_ref[...] * factor[:1]
        self.m_ref[...] = new
        self.l_ref[...] = total
        self.acc_ref[...] = attended

    def head_out(self, h, absorb_ref):
        columns = slice(h * ROWS, (h + 1) * ROWS)
        total = jnp.sum(self.l_ref[:, columns], axis=0, keepdims=True)
        attended = (self.acc_ref[:, columns] * (1.0 / total)).astype(BF16)
        return dot_first(absorb_ref[h], attended), self.m_ref[:1, columns] + jnp.log2(total)


def first_kernel(scale, own_ref, partner_ref, keys_ref, *state):
    half, chip, core, _ = position()

    @pl.when(half == 0)
    def _():
        rows = Rows(partner_ref, *state, scale)
        rows.chunk(keys_ref, 0, None, True)
        rows.chunk(keys_ref, 1, None, False)

    @pl.when(half == 1)
    def _():
        rows = Rows(own_ref, *state, scale)
        rows.chunk(keys_ref, 0, core, True)

        @pl.when(chip >= CHIPS // 2)
        def _():
            rows.chunk(keys_ref, 1, core, False)


def second_kernel(scale, partner_ref, keys_ref, absorb_ref, *refs):
    part_ref, *state = refs[3:]
    half = position()[0]

    @pl.when(half == 0)
    def _():
        rows = Rows(partner_ref, *state, scale)
        rows.chunk(keys_ref, 0, None, False)
        rows.chunk(keys_ref, 1, None, False)
        outs = [rows.head_out(h, absorb_ref) for h in range(HEADS)]
        for h, (out, _) in enumerate(outs):
            part_ref[h * VDIM : (h + 1) * VDIM, :] = out.astype(BF16)
        logs = jnp.concatenate([log for _, log in outs], axis=0)
        terms = [t.astype(F32) for t in thirds(logs)] + [jnp.zeros_like(logs)]
        part_ref[HEADS * VDIM :, :] = jnp.concatenate(terms, axis=0).astype(BF16)


def third_kernel(
    scale, own_ref, keys_ref, others_ref, values_ref, pattern_ref, absorb_ref, *refs
):
    out_ref, log_ref, dense_ref, *state = refs[3:]
    half, chip, core, _ = position()
    lower = half == 0
    rows = Rows(own_ref, *state, scale)

    def weights(*steps):
        for step in steps:
            columns = slice(step * COLS, (step + 1) * COLS)
            densify(values_ref.at[:, columns], pattern_ref.at[:, columns], dense_ref.at[:, columns])

    @pl.when(chip >= CHIPS // 2)
    def _():
        @pl.when(lower)
        def _():
            rows.chunk(keys_ref, 0, None, True)
            rows.chunk(keys_ref, 1, core, False)

        weights(0, 1)
        rows.chunk(others_ref, 0, None, False)
        weights(2, 3)
        rows.chunk(others_ref, 1, 1 - core, False)

    @pl.when(chip < CHIPS // 2)
    def _():
        @pl.when(lower)
        def _():
            rows.chunk(keys_ref, 0, core, True)

        weights(0, 1, 2, 3)
        rows.chunk(others_ref, 0, 1 - core, False)

    outs = [rows.head_out(h, absorb_ref) for h in range(HEADS)]
    for h, (out, _) in enumerate(outs):
        out_ref[h * VDIM : (h + 1) * VDIM, :] = out
    log_ref[...] = jnp.concatenate([log for _, log in outs], axis=0)


def output_kernel(mine_ref, log_ref, part_ref, down_ref, up_ref, dense_ref, out_ref):
    upper = position()[0]
    logs = part_ref[HEADS * VDIM :, :].astype(F32)
    logs = logs[:HEADS] + logs[HEADS : 2 * HEADS] + logs[2 * HEADS : 3 * HEADS]
    logs = jnp.where(upper == 1, logs, -jnp.inf)
    own_logs = log_ref[...]
    top = jnp.maximum(own_logs, logs)
    own_weights, weights = jnp.exp2(own_logs - top), jnp.exp2(logs - top)
    share = 1.0 / (own_weights + weights)
    own_weights, weights = own_weights * share, weights * share
    outs = []
    for h in range(HEADS):
        span = slice(h * VDIM, (h + 1) * VDIM)
        other = part_ref[span, :].astype(F32) * weights[h : h + 1]
        outs.append((mine_ref[span, :] * own_weights[h : h + 1] + other).astype(BF16))
    order = by_slot()
    flat = jnp.concatenate([dot_first(out, order).astype(BF16) for out in outs], axis=1)
    lowrank = dot(down_ref[...], jnp.concatenate(outs, axis=0))
    low = jnp.concatenate(thirds(lowrank.T), axis=1)
    for c in range(0, out_ref.shape[0], COLS):
        up = up_ref[:, c : c + COLS]
        terms = dot(flat, dense_ref[:, c : c + COLS])
        terms += dot(low, jnp.concatenate([up] * 3, axis=0))
        row = (c - FIRST * out_ref.shape[0] // HEADS) % out_ref.shape[0]
        out_ref[row : row + COLS, :] = terms.T.astype(BF16)


def sum_kernel(parts_ref, out_ref):
    total = parts_ref[0].astype(F32)
    for h in range(1, HEADS):
        total += parts_ref[h].astype(F32)
    out_ref[...] = total


def shape(*dims, dtype=F32):
    return jax.ShapeDtypeStruct(dims, dtype)


def params(mib):
    return pltpu.CompilerParams(vmem_limit_bytes=mib * MIB)


def cost(flops, nbytes, exps=0):
    return pl.CostEstimate(flops=flops, bytes_accessed=nbytes, transcendentals=exps)


VMEM = pl.BlockSpec(memory_space=pltpu.VMEM)
ANY = pl.BlockSpec(memory_space=pl.ANY)


def tables(positions):
    half = ROPE // 2
    freqs = 10000.0 ** (-jnp.arange(half, dtype=F32) / half)
    angles = positions.astype(F32)[:, None] * freqs
    cos, sin = jnp.cos(angles), jnp.sin(angles)
    return jnp.concatenate([cos, cos, -sin, sin], axis=1)


def local(
    tokens, kv_values, kv_pattern, kv_down, kv_up, kv_gain, queries, absorb_k, absorb_v,
    o_values, o_pattern, o_down, o_up,
):
    ctx = lax.axis_index("ctx")
    scale = LOG2E / math.sqrt(queries.shape[2])
    out_cols = o_values.shape[1]
    rank = o_down.shape[1]

    columns = jnp.transpose(queries, (1, 2, 0))
    partner = lax.ppermute(columns, "ctx", [(i + 2 * CHIPS, i) for i in range(2 * CHIPS)])

    raw = pl.pallas_call(
        project_kernel,
        out_shape=shape(HEADS, PIECE * WIDTH // 128, 128),
        in_specs=[ANY] * 5,
        out_specs=VMEM,
        scratch_shapes=[
            pltpu.VMEM(tokens.shape, BF16),
            pltpu.VMEM(kv_values.shape, BF16),
            pltpu.VMEM(kv_pattern.shape, jnp.int32),
            pltpu.VMEM(kv_down.shape[::-1], BF16),
            pltpu.VMEM(kv_up.shape, BF16),
            pltpu.VMEM((tokens.shape[1], WIDTH), BF16),
            pltpu.SemaphoreType.DMA((5,)),
        ],
        compiler_params=params(56),
        name="project",
    )(tokens, kv_values, kv_pattern, kv_down.T, kv_up)

    def exchange(x):
        return lax.all_to_all(x, "head", 0, 0, tiled=True, axis_index_groups=[list(PLACES)])

    parts = exchange(raw)

    positions = ctx * ROWS + jnp.arange(ROWS, dtype=jnp.int32)
    table = tables(positions)
    partner_table = tables(positions + 2 * CHIPS * ROWS)

    def query(x, t):
        return pl.pallas_call(
            query_kernel,
            out_shape=(shape(WIDTH, ALL, dtype=BF16), shape(8, 128)),
            in_specs=[VMEM] * 3,
            out_specs=(VMEM, VMEM),
            compiler_params=params(16),
            cost_estimate=cost(2 * ALL * NOPE * LAT, 4 * MIB),
            name="query",
        )(x, absorb_k, t.T)

    own_query, own_token = query(columns, table)
    partner_query, partner_token = query(partner, partner_table)

    piece = pl.pallas_call(
        finish_kernel,
        out_shape=shape(CHIPS, PIECE, WIDE, dtype=BF16),
        in_specs=[VMEM] * 4,
        out_specs=VMEM,
        compiler_params=params(16),
        name="finish",
    )(parts, kv_gain.reshape(1, LAT), table, own_token)

    along_z = [
        [(u * CHIPS + chip) * 2 + core for chip in ORDER]
        for u in range(2)
        for core in range(2)
    ]
    column = lax.all_to_all(piece, "ctx", 0, 0, tiled=True, axis_index_groups=along_z)
    packed = pl.pallas_call(
        pack_kernel,
        out_shape=shape(HEADS, PACKED, 128, dtype=BF16),
        in_specs=[VMEM] * 2,
        out_specs=VMEM,
        compiler_params=params(16),
        name="pack",
    )(column, partner_token)
    keys = exchange(packed)
    others = lax.ppermute(keys, "ctx", [(i, i ^ 1) for i in range(CTX)])

    state = (shape(8, ALL), shape(8, ALL), shape(LAT, ALL))
    scores = ALL * CHIPS * ROWS
    work = cost(2 * scores * (WIDTH + LAT), 8 * MIB, scores)
    first = pl.pallas_call(
        functools.partial(first_kernel, scale),
        out_shape=state,
        in_specs=[VMEM] * 3,
        out_specs=(VMEM,) * 3,
        compiler_params=params(20),
        cost_estimate=work,
        name="first",
    )(own_query, partner_query, keys)
    part, *second = pl.pallas_call(
        functools.partial(second_kernel, scale),
        out_shape=(shape(HEADS * VDIM + 4 * HEADS, ROWS, dtype=BF16),) + state,
        in_specs=[VMEM] * 6,
        out_specs=(VMEM,) * 4,
        input_output_aliases={3: 1, 4: 2, 5: 3},
        compiler_params=params(20),
        cost_estimate=work,
        name="second",
    )(partner_query, others, absorb_v, *first)
    received = lax.ppermute(part, "ctx", [(i, i + 2 * CHIPS) for i in range(2 * CHIPS)])
    mine, logs, dense, *_ = pl.pallas_call(
        functools.partial(third_kernel, scale),
        out_shape=(
            shape(HEADS * VDIM, ROWS),
            shape(HEADS, ROWS),
            shape(2 * o_values.shape[0], out_cols, dtype=BF16),
        )
        + state,
        in_specs=[VMEM] * 9,
        out_specs=(VMEM,) * 6,
        input_output_aliases={6: 3, 7: 4, 8: 5},
        compiler_params=params(20),
        cost_estimate=work,
        name="third",
    )(own_query, keys, others, o_values, o_pattern, absorb_v, *second)

    terms = pl.pallas_call(
        output_kernel,
        out_shape=shape(out_cols, ROWS, dtype=BF16),
        in_specs=[VMEM] * 6,
        out_specs=VMEM,
        compiler_params=params(20),
        cost_estimate=cost(2 * ROWS * HEADS * VDIM * out_cols, 8 * MIB),
        name="output",
    )(mine, logs, received, o_down.T, o_up, dense)
    shares = exchange(terms.reshape(HEADS, out_cols // HEADS, ROWS))
    return pl.pallas_call(
        sum_kernel,
        out_shape=shape(out_cols // HEADS, ROWS),
        in_specs=[VMEM],
        out_specs=VMEM,
        compiler_params=params(16),
        name="total",
    )(shares).T


def solution(mesh):
    in_specs = (
        P("ctx", "head"),
        P("head", None),
        P("head", None),
        P("head", None),
        P(),
        P(),
        P("ctx", "head", None),
        P("head", None, None),
        P("head", None, None),
        P("head", None),
        P("head", None),
        P("head", None),
        P(),
    )
    out_specs = P("ctx", "head")
    return jax.shard_map(local, mesh=mesh, in_specs=in_specs, out_specs=out_specs, check_vma=False)
```

```python
import functools
import math

import jax
import jax.numpy as jnp
from jax import lax
from jax.experimental import pallas as pl
from jax.experimental.pallas import tpu as pltpu
from jax.sharding import PartitionSpec as P

BF16 = jnp.bfloat16
F32 = jnp.float32
MIB = 1024 * 1024
HEADS = 8
ROWS = 128
ALL = HEADS * ROWS
PIECE = ROWS // HEADS
LAT = 512
ROPE = 64
WIDTH = LAT + ROPE
NOPE = 128
VDIM = 128
CTX = 32
CHIPS = 8
ORDER = (4, 5, 6, 7, 0, 1, 2, 3)
FIRST = 4
PLACES = tuple((place + FIRST) % HEADS for place in range(HEADS))
PACKED = ROWS * WIDTH // 128
HALF = ROWS // 2
KEYS = HEADS * HALF
WIDE = 640
UNSEEN = -1e30
COLS = 640
LOG2E = 1.4426950408889634


def dot(a, b):
    return jnp.dot(a, b, preferred_element_type=F32)


def dot_first(a, b):
    return lax.dot_general(a, b, (((0,), (0,)), ((), ())), preferred_element_type=F32)


def dot_last(a, b):
    return lax.dot_general(a, b, (((1,), (1,)), ((), ())), preferred_element_type=F32)


def unpair(count):
    half = count // 2
    rows = lax.broadcasted_iota(jnp.int32, (count, count), 0)
    columns = lax.broadcasted_iota(jnp.int32, (count, count), 1)
    wanted = jnp.where(rows < half, 2 * rows, 2 * (rows - half) + 1)
    return jnp.where(columns == wanted, 1.0, 0.0).astype(BF16)


def by_slot():
    rows = lax.broadcasted_iota(jnp.int32, (128, 128), 0)
    columns = lax.broadcasted_iota(jnp.int32, (128, 128), 1)
    return jnp.where(rows == 4 * (columns % 32) + columns // 32, 1.0, 0.0).astype(BF16)


def densify(values_ref, pattern_ref, dense_ref):
    total = values_ref.shape[0]
    zero = jnp.zeros((), BF16)
    begin = 0
    while begin < total:
        count = min(256, total - begin)
        half = count // 2
        pair = dot(unpair(count), values_ref[begin : begin + count, :]).astype(BF16)
        v0, v1 = pair[:half], pair[half:]
        p = pattern_ref[begin // 2 : begin // 2 + half, :].astype(BF16)
        is_0, is_1, is_3, is_5 = (p == jnp.asarray(k, BF16) for k in (0, 1, 3, 5))
        from_0 = p < jnp.asarray(3, BF16)
        later = jnp.where(from_0, zero, v0)
        to_2 = is_1 | is_3
        slots = (
            jnp.where(from_0, v0, zero),
            jnp.where(is_0, v1, jnp.where(is_5, zero, later)),
            jnp.where(to_2, v1, jnp.where(is_5, later, zero)),
            jnp.where(is_0 | to_2, zero, v1),
        )
        for k, slot in enumerate(slots):
            for b in range(half // 32):
                row = 2 * begin + 128 * b + 32 * k
                dense_ref[row : row + 32, :] = slot[32 * b : 32 * b + 32]
        begin += count


def position():
    ctx = lax.axis_index("ctx")
    return ctx >> 4, (ctx >> 1) & 7, ctx & 1, lax.axis_index("head")


def thirds(x):
    high = x.astype(BF16)
    rest = x - high.astype(F32)
    middle = rest.astype(BF16)
    low = (rest - middle.astype(F32)).astype(BF16)
    return high, middle, low


def project_kernel(
    tokens_hbm, values_hbm, pattern_hbm, down_hbm, up_hbm,
    raw_ref, tokens_ref, values_ref, pattern_ref, down_ref, up_ref, dense_ref, sems,
):
    copies = [
        pltpu.make_async_copy(source, target, sems.at[n])
        for n, (source, target) in enumerate(
            (
                (tokens_hbm, tokens_ref),
                (down_hbm, down_ref),
                (up_hbm, up_ref),
                (values_hbm, values_ref),
                (pattern_hbm, pattern_ref),
            )
        )
    ]
    for copy in copies:
        copy.start()
    for copy in copies[:3]:
        copy.wait()
    order = by_slot()
    tokens = tokens_ref[...]
    parts = [dot(tokens[:, b : b + 128], order).astype(BF16) for b in range(0, tokens.shape[1], 128)]
    low = jnp.concatenate(thirds(dot_last(tokens, down_ref[...])), axis=1)
    raw = dot(low, jnp.concatenate([up_ref[...]] * 3, axis=0))
    for copy in copies[3:]:
        copy.wait()
    densify(values_ref, pattern_ref, dense_ref)
    raw += dot(jnp.concatenate(parts, axis=1), dense_ref[...])
    for h in range(HEADS):
        piece = raw[PLACES[h] * PIECE : (PLACES[h] + 1) * PIECE]
        for c in range(LAT // 128):
            raw_ref[h, c * PIECE : (c + 1) * PIECE, :] = piece[:, c * 128 : (c + 1) * 128]
        rope = piece[:, LAT:]
        raw_ref[h, LAT // 128 * PIECE :, :] = jnp.concatenate(
            [rope[: PIECE // 2], rope[PIECE // 2 :]], axis=1
        )


def query_kernel(queries_ref, absorb_ref, table_ref, out_ref, token_ref):
    token_ref[...] = jnp.zeros(token_ref.shape, F32)
    half = ROPE // 2
    cos, sin = table_ref[:ROPE, :], table_ref[ROPE:, :]
    for h in range(HEADS):
        columns = slice(h * ROWS, (h + 1) * ROWS)
        out_ref[:LAT, columns] = dot_first(absorb_ref[h], queries_ref[h, :NOPE, :]).astype(BF16)
        x = queries_ref[h, NOPE:, :].astype(F32)
        swapped = jnp.concatenate([x[half:], x[:half]], axis=0)
        out_ref[LAT:, columns] = (x * cos + swapped * sin).astype(BF16)


def finish_kernel(parts_ref, gain_ref, table_ref, *refs):
    out_ref = refs[-1]
    raw = parts_ref[0]
    for h in range(1, HEADS):
        raw += parts_ref[h]
    latent = jnp.concatenate(
        [raw[c * PIECE : (c + 1) * PIECE] for c in range(LAT // 128)], axis=1
    )
    rope = raw[LAT // 128 * PIECE :]
    meansq = jnp.mean(latent * latent, axis=-1, keepdims=True)
    normed = (latent * lax.rsqrt(meansq + 1e-06) * gain_ref[...]).astype(BF16)
    table = table_ref[pl.ds(pl.multiple_of(position()[3] * PIECE, PIECE), PIECE), :]
    x = jnp.concatenate([rope[:, :ROPE], rope[:, ROPE:]], axis=0)
    half = ROPE // 2
    swapped = jnp.concatenate([x[:, half:], x[:, :half]], axis=1)
    turned = (x * table[:, :ROPE] + swapped * table[:, ROPE:]).astype(BF16)
    for c in range(CHIPS):
        out_ref[c, :, :LAT] = normed
        out_ref[c, :, LAT:WIDTH] = turned
        out_ref[c, :, WIDTH:] = jnp.zeros((PIECE, WIDE - WIDTH), BF16)


def pack_kernel(column_ref, *refs):
    out_ref = refs[-1]
    keys = jnp.concatenate([column_ref[ORDER.index(chip)] for chip in range(CHIPS)], axis=0)
    rope = keys[:, LAT:WIDTH]
    rope = jnp.concatenate([rope[: ROWS // 2], rope[ROWS // 2 :]], axis=1)
    for k in range(HEADS):
        for c in range(LAT // 128):
            out_ref[k, c * ROWS : (c + 1) * ROWS, :] = keys[:, c * 128 : (c + 1) * 128]
        out_ref[k, LAT // 128 * ROWS :, :] = rope


def unpack(keys_ref, part):
    latents, ropes = [], []
    for k in range(HEADS):
        rows = [c * ROWS + part * HALF for c in range(LAT // 128)]
        latents.append(jnp.concatenate([keys_ref[k, r : r + HALF, :] for r in rows], axis=1))
        ropes.append(keys_ref[k, LAT // 128 * ROWS :, part * ROPE : (part + 1) * ROPE])
    return jnp.concatenate(latents, axis=0), jnp.concatenate(ropes, axis=0)


class Rows:
    def __init__(self, q_ref, m_ref, l_ref, acc_ref, scale):
        _, self.chip, self.core, _ = position()
        self.q_ref, self.m_ref, self.l_ref, self.acc_ref = q_ref, m_ref, l_ref, acc_ref
        self.scale = scale

    def chunk(self, keys_ref, part, key_core, fresh):
        latent, rope = unpack(keys_ref, part)
        scores = dot(jnp.concatenate([latent, rope], axis=1), self.q_ref[...]) * self.scale
        if key_core is not None:
            query = lax.broadcasted_iota(jnp.int32, (1, ALL), 1) % ROWS
            key = lax.broadcasted_iota(jnp.int32, (KEYS, 1), 0)
            ahead = (2 * self.chip + self.core) * ROWS + query
            place = (2 * (part * CHIPS // 2 + key % HALF // PIECE) + key_core) * ROWS
            place += (key // HALF + FIRST) % HEADS * PIECE + key % PIECE
            scores = jnp.where(place <= ahead, scores, UNSEEN)
        top = jnp.max(scores, axis=0, keepdims=True)
        new = jnp.broadcast_to(top, (8, ALL)) if fresh else jnp.maximum(self.m_ref[...], top)
        weights = jnp.exp2(scores - new[:1])
        total = jnp.sum(weights.reshape(KEYS // 8, 8, ALL), axis=0)
        attended = dot(latent.T, weights.astype(BF16))
        if not fresh:
            factor = jnp.exp2(self.m_ref[...] - new)
            total += self.l_ref[...] * factor
            attended += self.acc_ref[...] * factor[:1]
        self.m_ref[...] = new
        self.l_ref[...] = total
        self.acc_ref[...] = attended

    def head_out(self, h, absorb_ref):
        columns = slice(h * ROWS, (h + 1) * ROWS)
        total = jnp.sum(self.l_ref[:, columns], axis=0, keepdims=True)
        attended = (self.acc_ref[:, columns] * (1.0 / total)).astype(BF16)
        return dot_first(absorb_ref[h], attended), self.m_ref[:1, columns] + jnp.log2(total)


def first_kernel(scale, own_ref, partner_ref, keys_ref, *state):
    half, chip, core, _ = position()

    @pl.when(half == 0)
    def _():
        rows = Rows(partner_ref, *state, scale)
        rows.chunk(keys_ref, 0, None, True)
        rows.chunk(keys_ref, 1, None, False)

    @pl.when(half == 1)
    def _():
        rows = Rows(own_ref, *state, scale)
        rows.chunk(keys_ref, 0, core, True)

        @pl.when(chip >= CHIPS // 2)
        def _():
            rows.chunk(keys_ref, 1, core, False)


def second_kernel(scale, partner_ref, keys_ref, absorb_ref, *refs):
    part_ref, *state = refs[3:]
    half = position()[0]

    @pl.when(half == 0)
    def _():
        rows = Rows(partner_ref, *state, scale)
        rows.chunk(keys_ref, 0, None, False)
        rows.chunk(keys_ref, 1, None, False)
        outs = [rows.head_out(h, absorb_ref) for h in range(HEADS)]
        for h, (out, _) in enumerate(outs):
            part_ref[h * VDIM : (h + 1) * VDIM, :] = out.astype(BF16)
        logs = jnp.concatenate([log for _, log in outs], axis=0)
        terms = [t.astype(F32) for t in thirds(logs)] + [jnp.zeros_like(logs)]
        part_ref[HEADS * VDIM :, :] = jnp.concatenate(terms, axis=0).astype(BF16)


def third_kernel(
    scale, own_ref, keys_ref, others_ref, values_ref, pattern_ref, absorb_ref, *refs
):
    out_ref, log_ref, dense_ref, *state = refs[3:]
    half, chip, core, _ = position()
    lower = half == 0
    rows = Rows(own_ref, *state, scale)

    def weights(*steps):
        for step in steps:
            columns = slice(step * COLS, (step + 1) * COLS)
            densify(values_ref.at[:, columns], pattern_ref.at[:, columns], dense_ref.at[:, columns])

    @pl.when(chip >= CHIPS // 2)
    def _():
        @pl.when(lower)
        def _():
            rows.chunk(keys_ref, 0, None, True)
            rows.chunk(keys_ref, 1, core, False)

        weights(0, 1)
        rows.chunk(others_ref, 0, None, False)
        weights(2, 3)
        rows.chunk(others_ref, 1, 1 - core, False)

    @pl.when(chip < CHIPS // 2)
    def _():
        @pl.when(lower)
        def _():
            rows.chunk(keys_ref, 0, core, True)

        weights(0, 1, 2, 3)
        rows.chunk(others_ref, 0, 1 - core, False)

    outs = [rows.head_out(h, absorb_ref) for h in range(HEADS)]
    for h, (out, _) in enumerate(outs):
        out_ref[h * VDIM : (h + 1) * VDIM, :] = out
    log_ref[...] = jnp.concatenate([log for _, log in outs], axis=0)


def output_kernel(mine_ref, log_ref, part_ref, down_ref, up_ref, dense_ref, out_ref):
    upper = position()[0]
    logs = part_ref[HEADS * VDIM :, :].astype(F32)
    logs = logs[:HEADS] + logs[HEADS : 2 * HEADS] + logs[2 * HEADS : 3 * HEADS]
    logs = jnp.where(upper == 1, logs, -jnp.inf)
    own_logs = log_ref[...]
    top = jnp.maximum(own_logs, logs)
    own_weights, weights = jnp.exp2(own_logs - top), jnp.exp2(logs - top)
    share = 1.0 / (own_weights + weights)
    own_weights, weights = own_weights * share, weights * share
    outs = []
    for h in range(HEADS):
        span = slice(h * VDIM, (h + 1) * VDIM)
        other = part_ref[span, :].astype(F32) * weights[h : h + 1]
        outs.append((mine_ref[span, :] * own_weights[h : h + 1] + other).astype(BF16))
    order = by_slot()
    flat = jnp.concatenate([dot_first(out, order).astype(BF16) for out in outs], axis=1)
    lowrank = dot(down_ref[...], jnp.concatenate(outs, axis=0))
    low = jnp.concatenate(thirds(lowrank.T), axis=1)
    for c in range(0, out_ref.shape[0], COLS):
        up = up_ref[:, c : c + COLS]
        terms = dot(flat, dense_ref[:, c : c + COLS])
        terms += dot(low, jnp.concatenate([up] * 3, axis=0))
        row = (c - FIRST * out_ref.shape[0] // HEADS) % out_ref.shape[0]
        out_ref[row : row + COLS, :] = terms.T.astype(BF16)


def shape(*dims, dtype=F32):
    return jax.ShapeDtypeStruct(dims, dtype)


def params(mib):
    return pltpu.CompilerParams(vmem_limit_bytes=mib * MIB)


def cost(flops, nbytes, exps=0):
    return pl.CostEstimate(flops=flops, bytes_accessed=nbytes, transcendentals=exps)


VMEM = pl.BlockSpec(memory_space=pltpu.VMEM)
ANY = pl.BlockSpec(memory_space=pl.ANY)


def tables(positions):
    half = ROPE // 2
    freqs = 10000.0 ** (-jnp.arange(half, dtype=F32) / half)
    angles = positions.astype(F32)[:, None] * freqs
    cos, sin = jnp.cos(angles), jnp.sin(angles)
    return jnp.concatenate([cos, cos, -sin, sin], axis=1)


def local(
    tokens, kv_values, kv_pattern, kv_down, kv_up, kv_gain, queries, absorb_k, absorb_v,
    o_values, o_pattern, o_down, o_up,
):
    ctx = lax.axis_index("ctx")
    scale = LOG2E / math.sqrt(queries.shape[2])
    out_cols = o_values.shape[1]
    rank = o_down.shape[1]

    columns = jnp.transpose(queries, (1, 2, 0))
    partner = lax.ppermute(columns, "ctx", [(i + 2 * CHIPS, i) for i in range(2 * CHIPS)])

    raw = pl.pallas_call(
        project_kernel,
        out_shape=shape(HEADS, PIECE * WIDTH // 128, 128),
        in_specs=[ANY] * 5,
        out_specs=VMEM,
        scratch_shapes=[
            pltpu.VMEM(tokens.shape, BF16),
            pltpu.VMEM(kv_values.shape, BF16),
            pltpu.VMEM(kv_pattern.shape, jnp.int32),
            pltpu.VMEM(kv_down.shape[::-1], BF16),
            pltpu.VMEM(kv_up.shape, BF16),
            pltpu.VMEM((tokens.shape[1], WIDTH), BF16),
            pltpu.SemaphoreType.DMA((5,)),
        ],
        compiler_params=params(56),
        name="project",
    )(tokens, kv_values, kv_pattern, kv_down.T, kv_up)

    def exchange(x):
        return lax.all_to_all(x, "head", 0, 0, tiled=True, axis_index_groups=[list(PLACES)])

    parts = exchange(raw)

    positions = ctx * ROWS + jnp.arange(ROWS, dtype=jnp.int32)
    table = tables(positions)
    partner_table = tables(positions + 2 * CHIPS * ROWS)

    def query(x, t):
        return pl.pallas_call(
            query_kernel,
            out_shape=(shape(WIDTH, ALL, dtype=BF16), shape(8, 128)),
            in_specs=[VMEM] * 3,
            out_specs=(VMEM, VMEM),
            compiler_params=params(16),
            cost_estimate=cost(2 * ALL * NOPE * LAT, 4 * MIB),
            name="query",
        )(x, absorb_k, t.T)

    own_query, own_token = query(columns, table)
    partner_query, partner_token = query(partner, partner_table)

    piece = pl.pallas_call(
        finish_kernel,
        out_shape=shape(CHIPS, PIECE, WIDE, dtype=BF16),
        in_specs=[VMEM] * 3,
        out_specs=VMEM,
        compiler_params=params(16),
        name="finish",
    )(parts, kv_gain.reshape(1, LAT), table)

    along_z = [
        [(u * CHIPS + chip) * 2 + core for chip in ORDER]
        for u in range(2)
        for core in range(2)
    ]
    column = lax.all_to_all(piece, "ctx", 0, 0, tiled=True, axis_index_groups=along_z)
    packed = pl.pallas_call(
        pack_kernel,
        out_shape=shape(HEADS, PACKED, 128, dtype=BF16),
        in_specs=[VMEM] * 3,
        out_specs=VMEM,
        compiler_params=params(16),
        name="pack",
    )(column, own_token, partner_token)
    keys = exchange(packed)
    others = lax.ppermute(keys, "ctx", [(i, i ^ 1) for i in range(CTX)])

    state = (shape(8, ALL), shape(8, ALL), shape(LAT, ALL))
    scores = ALL * CHIPS * ROWS
    work = cost(2 * scores * (WIDTH + LAT), 8 * MIB, scores)
    first = pl.pallas_call(
        functools.partial(first_kernel, scale),
        out_shape=state,
        in_specs=[VMEM] * 3,
        out_specs=(VMEM,) * 3,
        compiler_params=params(20),
        cost_estimate=work,
        name="first",
    )(own_query, partner_query, keys)
    part, *second = pl.pallas_call(
        functools.partial(second_kernel, scale),
        out_shape=(shape(HEADS * VDIM + 4 * HEADS, ROWS, dtype=BF16),) + state,
        in_specs=[VMEM] * 6,
        out_specs=(VMEM,) * 4,
        input_output_aliases={3: 1, 4: 2, 5: 3},
        compiler_params=params(20),
        cost_estimate=work,
        name="second",
    )(partner_query, others, absorb_v, *first)
    received = lax.ppermute(part, "ctx", [(i, i + 2 * CHIPS) for i in range(2 * CHIPS)])
    mine, logs, dense, *_ = pl.pallas_call(
        functools.partial(third_kernel, scale),
        out_shape=(
            shape(HEADS * VDIM, ROWS),
            shape(HEADS, ROWS),
            shape(2 * o_values.shape[0], out_cols, dtype=BF16),
        )
        + state,
        in_specs=[VMEM] * 9,
        out_specs=(VMEM,) * 6,
        input_output_aliases={6: 3, 7: 4, 8: 5},
        compiler_params=params(20),
        cost_estimate=work,
        name="third",
    )(own_query, keys, others, o_values, o_pattern, absorb_v, *second)

    terms = pl.pallas_call(
        output_kernel,
        out_shape=shape(out_cols, ROWS, dtype=BF16),
        in_specs=[VMEM] * 6,
        out_specs=VMEM,
        compiler_params=params(20),
        cost_estimate=cost(2 * ROWS * HEADS * VDIM * out_cols, 8 * MIB),
        name="output",
    )(mine, logs, received, o_down.T, o_up, dense)
    shares = exchange(terms.reshape(HEADS, out_cols // HEADS, ROWS))
    return jnp.sum(shares.astype(F32), axis=0).T


def solution(mesh):
    in_specs = (
        P("ctx", "head"),
        P("head", None),
        P("head", None),
        P("head", None),
        P(),
        P(),
        P("ctx", "head", None),
        P("head", None, None),
        P("head", None, None),
        P("head", None),
        P("head", None),
        P("head", None),
        P(),
    )
    out_specs = P("ctx", "head")
    return jax.shard_map(local, mesh=mesh, in_specs=in_specs, out_specs=out_specs, check_vma=False)
```
